128 devices in a mesh: gx: 32 (over z, x, core), gy: 4 (over y).
Axes of the slice: x: 4, y: 4, z: 4, core: 2. Of those that a mesh axis runs over, the one named last changes fastest.
Arguments:
- populations: float32 [19, 1024, 2048], P(None, 'gx', 'gy'), may hold values from 0 to 0.7, as said below
- positions: float32 [3072, 3, 642], P(('gx', 'gy')), may hold values from -3 to 31, as said below
- stiffness: float32 [3072], P(('gx', 'gy')), may hold values from 0.002 to 0.02
- membrane_shape: float32 [3, 642], replicated, may hold values from -6 to 6
- neighbours: int32 [642, 6], replicated, may hold values from 0 to 641, as said below
- home_tile: int32 [3072], P(('gx', 'gy')), may hold values from 0 to 127, as said below
Outputs:
- populations_out: float32 [19, 1024, 2048], P(None, 'gx', 'gy')
- displacement: float32 [3072, 3, 642], P(('gx', 'gy'))
- force_density: float32 [3, 1024, 2048], P(None, 'gx', 'gy')
The draws below stay inside these ranges and needn't reach their ends.
Inputs may be any that keep to these rules, and one draw needn't show every extreme that they name: `populations`: every entry is positive. `positions`: the first coordinate lies within [1, 31], the second within [1, 31]; the third is taken modulo 16. `neighbours`: row v never names v. `home_tile`: cells are owned in blocks of 24 in gx+gy order; the home tile of a cell owned at gx index a has gx index a - 1, a or a + 1 (cyclically) and any gy index, numbered gx index times the number of gy devices plus gy index; at most 4 cells of one device share a home tile, and in every device some home tile has exactly 4 of them.
All inputs are finite; a program needn't handle non-finite values.
Results may differ from the reference program's by a relative error of at most 0.0022.
Values sent between devices are 32-bit elements; how exact they have to be, the bound alone decides.
A program may use at most 64 MiB of HBM per device.

```python
import math
import jax
import jax.numpy as jnp
from jax import lax

CX = 32
CY = 32
CZ = 16
V = 642
NB = 6
CELL_DEV = 24
CAP = 4
STEPS = 2
NX = 1024
NY = 128
NCELL = 3072
N_GX = 32
N_GY = 4


LATTICE_WEIGHT = [1.0 / 3.0] + [1.0 / 18.0] * 6 + [1.0 / 36.0] * 12


def draw_populations(key, part):
    weights = jnp.asarray(LATTICE_WEIGHT, jnp.float32)[:, None, None]
    full_shape = (19, NX, NY * CZ)
    roughness = jax.random.uniform(key, full_shape, jnp.float32, 0.2, 1.8)
    return weights * roughness


def draw_positions(key, part):
    subkeys = jax.random.split(key, 2)
    lowest = jnp.asarray([4.0, 4.0, 0.0], jnp.float32)[:, None]
    highest = jnp.asarray([CX - 4.0, CY - 4.0, CZ * 1.0], jnp.float32)[:, None]
    centers = lowest + (highest - lowest) * jax.random.uniform(subkeys[0], (NCELL, 3, 1), jnp.float32)
    scatter_noise = jax.random.uniform(subkeys[1], (NCELL, 3, V), jnp.float32, -1.0, 1.0)
    return centers + 3.0 * scatter_noise


def draw_neighbours(key, part):
    hopping = jax.random.randint(key, (V, NB), 1, V, jnp.int32)
    return (jnp.arange(V, dtype=jnp.int32)[:, None] + hopping) % V


def draw_home_tile(key, part):
    slots_total = 3 * N_GY * CAP

    def one_owner(owner):
        subkeys = jax.random.split(jax.random.fold_in(key, owner), 3)
        full_group = jax.random.randint(subkeys[0], (), 0, 3 * N_GY, jnp.int32)
        scores = jax.random.permutation(subkeys[1], slots_total).astype(jnp.int32)
        groups = jnp.arange(slots_total, dtype=jnp.int32) // CAP
        scores = jnp.where(groups == full_group, scores - slots_total, scores)
        chosen = jnp.argsort(scores)[:CELL_DEV].astype(jnp.int32)
        chosen = jax.random.permutation(subkeys[2], chosen)
        group = chosen // CAP
        offset = group // N_GY
        target_y = group % N_GY
        owner_x = owner // N_GY
        return (owner_x + offset - 1) % N_GX * N_GY + target_y
    return jax.vmap(one_owner)(jnp.arange(N_GX * N_GY, dtype=jnp.int32)).reshape(-1)


def steps_of(rng, dims, pieces, low, high):
    level = 1.0
    for position, shards_of in pieces:
        draws = jax.random.uniform(jax.random.fold_in(jax.random.fold_in(rng, 6), position), (shards_of,), jnp.float32, low / len(pieces), high / len(pieces))
        level = level * jnp.repeat(jnp.exp(draws), dims[position] // shards_of).reshape((-1,) + (1,) * (len(dims) - 1 - position))
    return level


def bell_draw(key, dims, spread, limit, kind=jnp.bfloat16):
    values = jax.random.normal(key, dims, jnp.float32) * spread
    return jnp.minimum(jnp.maximum(values, -limit), limit).astype(kind)


def setup_inputs(seed: int = 0) -> dict:
    key_list = jax.random.split(jax.random.key(seed), 7)
    return {
        "populations": draw_populations(jax.random.fold_in(key_list[6], 71), 0),
        "positions": draw_positions(jax.random.fold_in(key_list[6], 71), 0),
        "stiffness": jnp.clip(jnp.exp(math.log(0.02) - 2.30258502 * jax.random.uniform(key_list[2], (NCELL,), jnp.float32) ** steps_of(key_list[2], (NCELL,), ((0, 128),), -0.2, 0.2)), 0.002, 0.02),
        "membrane_shape": bell_draw(key_list[3], (3, V), 1.5, 6.0, jnp.float32),
        "neighbours": draw_neighbours(jax.random.fold_in(key_list[6], 71), 0),
        "home_tile": draw_home_tile(jax.random.fold_in(key_list[6], 71), 0),
    }


LATTICE_VELOCITY = [[0, 0, 0], [1, 0, 0], [-1, 0, 0], [0, 1, 0], [0, -1, 0], [0, 0, 1], [0, 0, -1], [1, 1, 0], [-1, -1, 0], [1, -1, 0], [-1, 1, 0], [1, 0, 1], [-1, 0, -1], [1, 0, -1], [-1, 0, 1], [0, 1, 1], [0, -1, -1], [0, 1, -1], [0, -1, 1]]
LATTICE_WEIGHT = [1.0 / 3.0] + [1.0 / 18.0] * 6 + [1.0 / 36.0] * 12
RELAX_RATE = 1.25
PUSH_SCALE = 0.05
TETHER_GAIN = 2.0


def stiffness_matrix(neighbours):
    vertices = neighbours.shape[0]
    columns = jnp.arange(vertices, dtype=jnp.int32)
    linked = jnp.sum((neighbours[:, :, None] == columns[None, None, :]).astype(jnp.float32), axis=1)
    linked = linked + linked.T
    degree = jnp.sum(linked, axis=1)
    return jnp.diag(degree + TETHER_GAIN) - linked


def membrane_force(places, stiffness, membrane_shape, matrix):
    center = jnp.mean(places, axis=2, keepdims=True)
    strain = places - center - membrane_shape[None]
    vertices = places.shape[2]
    pulled = jnp.dot(strain.reshape(-1, vertices), matrix, precision=lax.Precision.HIGHEST, preferred_element_type=jnp.float32)
    return -stiffness[:, None, None] * pulled.reshape(places.shape)


def moments(populations):
    velocity_table = jnp.asarray(LATTICE_VELOCITY, jnp.float32)
    density = jnp.sum(populations, axis=0)
    momentum = jnp.tensordot(velocity_table.T, populations, axes=1, precision=lax.Precision.HIGHEST)
    return density, momentum


def fluid_velocity(populations, push):
    density, momentum = moments(populations)
    return (momentum + 0.5 * push) / density


def collide(populations, push):
    velocity_table = jnp.asarray(LATTICE_VELOCITY, jnp.float32)
    weights = jnp.asarray(LATTICE_WEIGHT, jnp.float32)[:, None, None]
    density, momentum = moments(populations)
    velocity = (momentum + 0.5 * push) / density
    along = jnp.tensordot(velocity_table, velocity, axes=1, precision=lax.Precision.HIGHEST)
    push_along = jnp.tensordot(velocity_table, push, axes=1, precision=lax.Precision.HIGHEST)
    speed_square = jnp.sum(velocity * velocity, axis=0)
    push_dot = jnp.sum(velocity * push, axis=0)
    balance = weights * density * (1.0 + 3.0 * along + 4.5 * along * along - 1.5 * speed_square)
    source = (1.0 - 0.5 * RELAX_RATE) * weights * (3.0 * (push_along - push_dot) + 9.0 * along * push_along)
    return populations - RELAX_RATE * (populations - balance) + source


def stream_all(post):
    shaped = post.reshape(19, NX, NY, CZ)
    moved = [jnp.roll(shaped[member], tuple(LATTICE_VELOCITY[member]), axis=(0, 1, 2)) for member in range(19)]
    return jnp.stack(moved).reshape(post.shape)


def axis_hats(coordinate, extent):
    floored = jnp.floor(coordinate)
    fraction = coordinate - floored
    base_index = floored.astype(jnp.int32)
    hat_pairs = []
    for advance, weight in ((0, 1.0 - fraction), (1, fraction)):
        corner = base_index + advance
        inside = (corner >= 0) & (corner < extent)
        hat_pairs.append((jnp.clip(corner, 0, extent - 1), jnp.where(inside, weight, 0.0)))
    return hat_pairs


def periodic_hats(coordinate, extent):
    wrapped = jnp.mod(coordinate, extent * 1.0)
    floored = jnp.floor(wrapped)
    fraction = wrapped - floored
    base_index = floored.astype(jnp.int32)
    return [(base_index % extent, 1.0 - fraction), ((base_index + 1) % extent, fraction)]


def rounded(values):
    return lax.optimization_barrier(values.astype(jnp.bfloat16)).astype(jnp.float32)


def tile_corners(places, home_tile):
    tile_x = home_tile // N_GY
    tile_y = home_tile % N_GY
    anchor_x = (tile_x * CX)[:, None]
    anchor_y = (tile_y * CY)[:, None]
    x_hats = axis_hats(places[:, 0], CX)
    y_hats = axis_hats(places[:, 1], CY)
    z_hats = periodic_hats(places[:, 2], CZ)
    plane_pairs = []
    for y_index, y_weight in y_hats:
        for z_index, z_weight in z_hats:
            table = rounded(y_weight * z_weight)
            columns = ((anchor_y + y_index) * CZ + z_index).reshape(-1)
            plane_pairs.append((columns, table))
    row_pairs = [((anchor_x + x_index).reshape(-1), x_weight) for x_index, x_weight in x_hats]
    return row_pairs, plane_pairs


def spread_all(places, force, home_tile):
    row_pairs, plane_pairs = tile_corners(places, home_tile)
    grid = jnp.zeros((3, NX, NY * CZ), jnp.float32)
    for rows, x_weight in row_pairs:
        lifted = rounded(force * x_weight[:, None, :])
        for columns, table in plane_pairs:
            values = (lifted * table[:, None, :]).transpose(1, 0, 2).reshape(3, -1)
            grid = grid.at[:, rows, columns].add(values)
    return grid


def sample_all(places, velocity, home_tile):
    row_pairs, plane_pairs = tile_corners(places, home_tile)
    count_cells = places.shape[0]
    vertices = places.shape[2]
    result = jnp.zeros(places.shape, jnp.float32)
    for rows, x_weight in row_pairs:
        inner = jnp.zeros((3, count_cells * vertices), jnp.float32)
        for columns, table in plane_pairs:
            inner = inner + velocity[:, rows, columns].astype(jnp.float32) * table.reshape(-1)[None]
        result = result + x_weight[:, None, :] * inner.reshape(3, count_cells, vertices).transpose(1, 0, 2)
    return result


def reference(populations, positions, stiffness, membrane_shape, neighbours, home_tile):
    matrix = stiffness_matrix(neighbours)
    starting = positions
    density_grid = jnp.zeros((3, NX, NY * CZ), jnp.float32)
    for _ in range(STEPS):
        force = membrane_force(positions, stiffness, membrane_shape, matrix)
        density_grid = spread_all(positions, force, home_tile)
        push = PUSH_SCALE * density_grid
        populations = stream_all(collide(populations, push))
        velocity = fluid_velocity(populations, push).astype(jnp.bfloat16)
        positions = positions + sample_all(positions, velocity, home_tile)
    return populations, positions - starting, density_grid
```

```python
import functools

import jax
import jax.numpy as jnp
from jax import lax
from jax.experimental import pallas as pl
from jax.experimental.pallas import tpu as pltpu
from jax.sharding import PartitionSpec as P

CZ = 16
CAP = 4
STEPS = 2
GROUPS = 12
SELF = 4
WIDE = 768
MAIN = 640
LANES = CAP * MAIN + 128
CHUNKS = [(0, 512), (512, 512), (1024, 512), (1536, 512), (2048, 512), (2560, 128)]

VELOCITY = [
    (0, 0, 0),
    (1, 0, 0),
    (-1, 0, 0),
    (0, 1, 0),
    (0, -1, 0),
    (0, 0, 1),
    (0, 0, -1),
    (1, 1, 0),
    (-1, -1, 0),
    (1, -1, 0),
    (-1, 1, 0),
    (1, 0, 1),
    (-1, 0, -1),
    (1, 0, -1),
    (-1, 0, 1),
    (0, 1, 1),
    (0, -1, -1),
    (0, 1, -1),
    (0, -1, 1),
]
WEIGHT = [1.0 / 3.0] + [1.0 / 18.0] * 6 + [1.0 / 36.0] * 12
RIGHT_MOVERS = [1, 7, 9, 11, 13]
LEFT_MOVERS = [2, 8, 10, 12, 14]
UPWARD_MOVERS = [3, 7, 10, 15, 17]
DOWNWARD_MOVERS = [4, 8, 9, 16, 18]
EDGE_MOVERS = [(7, 24, 384), (8, 0, 0), (9, 24, 0), (10, 0, 384)]
RELAX_RATE = 1.25
PUSH_SCALE = 0.05
TETHER_GAIN = 2.0
MESH = pl.DeviceIdType.MESH
F32 = jnp.float32
BF16 = jnp.bfloat16


def signed_sum(parts):
    total = None
    for sign, value in parts:
        if sign == 0:
            continue
        if total is None:
            total = value if sign > 0 else -value
        else:
            total = total + value if sign > 0 else total - value
    return total


def moments(f):
    density = f[0]
    for q in range(1, 19):
        density = density + f[q]
    momentum = [signed_sum([(VELOCITY[q][c], f[q]) for q in range(1, 19)]) for c in range(3)]
    return density, momentum


def hat(row, count, first):
    grid = lax.broadcasted_iota(jnp.int32, (count, row.shape[1]), 0).astype(F32) + first
    return jnp.maximum(0.0, 1.0 - jnp.abs(row - grid))


def hat_z(row):
    wrapped = row - CZ * jnp.floor(row * (1.0 / CZ))
    grid = lax.broadcasted_iota(jnp.int32, (CZ, row.shape[1]), 0).astype(F32)
    gap = jnp.abs(wrapped - grid)
    return jnp.maximum(0.0, 1.0 - jnp.minimum(gap, CZ - gap))


def kernel(
    nx,
    ny,
    source_ref,
    stiff_ref,
    slot_ref,
    pops_ref,
    places_ref,
    shape_ref,
    near_ref,
    pops_out,
    moved_out,
    density_out,
    sendbuf,
    cells,
    drift,
    returned,
    matrix32,
    matrix,
    diagonal,
    shapes,
    forces,
    flat,
    table,
    lifted,
    total,
    post,
    velocity,
    x_send,
    y_send,
    e_send,
    x_recv,
    y_recv,
    e_recv,
    cell_send_sem,
    cell_recv_sem,
    back_send_sem,
    back_recv_sem,
    halo_send_sem,
    halo_recv_sem,
):
    me_x = lax.axis_index("gx")
    me_y = lax.axis_index("gy")
    vertices = places_ref.shape[2]

    def away(dx, dy):
        return (lax.rem(me_x + dx + nx, nx), lax.rem(me_y + dy + ny, ny))

    barrier = pltpu.get_barrier_semaphore()
    for g in range(GROUPS):
        if g != SELF:
            pl.semaphore_signal(barrier, inc=1, device_id=away(g // 4 - 1, g % 4), device_id_type=MESH)

    for g in range(GROUPS):
        into = cells if g == SELF else sendbuf
        into[g, 8:16, :] = jnp.zeros((8, WIDE), F32)
        for r in range(CAP):
            s = g * CAP + r
            into[g, 3 * r : 3 * r + 3, MAIN:WIDE] = jnp.full((3, 128), stiff_ref[s], F32)
            into[g, 3 * r : 3 * r + 3, 0:vertices] = places_ref[source_ref[s]]
    pl.semaphore_wait(barrier, GROUPS - 1)

    def cell_copy(g):
        return pltpu.make_async_remote_copy(
            src_ref=sendbuf.at[g],
            dst_ref=cells.at[g],
            send_sem=cell_send_sem.at[g],
            recv_sem=cell_recv_sem.at[g],
            device_id=away(g // 4 - 1, g % 4),
            device_id_type=MESH,
        )

    def back_copy(g):
        return pltpu.make_async_remote_copy(
            src_ref=drift.at[g],
            dst_ref=returned.at[g],
            send_sem=back_send_sem.at[g],
            recv_sem=back_recv_sem.at[g],
            device_id=away(1 - g // 4, ny - g % 4),
            device_id_type=MESH,
        )

    for g in (5, 7, 6, 0, 8, 1, 3, 9, 11, 2, 10):
        cell_copy(g).start()

    def link_rows(b, _):
        first = pl.multiple_of(b * 8, 8)
        rows = lax.broadcasted_iota(jnp.int32, (8, WIDE), 0) + first
        count = jnp.zeros((8, WIDE), F32)
        for n in range(6):
            count = count + jnp.where(near_ref[n : n + 1, :] == rows, 1.0, 0.0)
        matrix32[pl.ds(first, 8), :] = count
        return 0

    lax.fori_loop(0, WIDE // 8, link_rows, 0)
    degree = jnp.zeros((1, WIDE), F32)
    for b in range(WIDE // 128):
        both = matrix32[128 * b : 128 * b + 128, :] + matrix32[:, 128 * b : 128 * b + 128].T
        matrix[128 * b : 128 * b + 128, :] = both.astype(BF16)
        degree = degree + jnp.sum(both, axis=0, keepdims=True)
    inside = lax.broadcasted_iota(jnp.int32, (1, WIDE), 1) < vertices
    diagonal[...] = jnp.where(inside, degree + TETHER_GAIN, 0.0)
    shapes[...] = jnp.zeros_like(shapes)
    for r in range(CAP):
        shapes[3 * r : 3 * r + 3, 0:vertices] = shape_ref[...]

    def batch_force(b):
        x = cells[pl.ds(4 * b, 4)].reshape(64, WIDE)
        keep = lax.broadcasted_iota(jnp.int32, (64, WIDE), 1) < vertices
        center = jnp.sum(jnp.where(keep, x, 0.0), axis=1, keepdims=True) * (1.0 / vertices)
        shape = jnp.concatenate([shapes[...]] * 4, axis=0)
        strain = jnp.where(keep, x - center - shape, 0.0)
        high = strain.astype(BF16)
        rest = strain - high.astype(F32)
        middle = rest.astype(BF16)
        low = (rest - middle.astype(F32)).astype(BF16)
        parts = jnp.dot(
            jnp.concatenate([high, middle, low], axis=0), matrix[...], preferred_element_type=F32
        )
        linked = parts[0:64] + parts[64:128] + parts[128:192]
        pulled = strain * diagonal[...] - linked
        forces[...] = (-x[:, vertices : vertices + 1] * pulled).reshape(4, 16, WIDE)

    def flatten(block, into, g, row):
        lane = lax.broadcasted_iota(jnp.int32, (1, 128), 1)
        for c in range(3):
            tail = jnp.zeros((1, 128), F32)
            for r in range(CAP):
                into[g, row + c : row + c + 1, MAIN * r : MAIN * r + MAIN] = block[
                    3 * r + c : 3 * r + c + 1, 0:MAIN
                ]
                end = block[3 * r + c : 3 * r + c + 1, MAIN:WIDE]
                if r:
                    end = pltpu.roll(end, 2 * r, 1)
                tail = jnp.where((lane >= 2 * r) & (lane < 2 * r + 2), end, tail)
            into[g, row + c : row + c + 1, MAIN * CAP : LANES] = tail

    def spread_group(b, k):
        g = 4 * b + k
        flatten(cells[g], flat, g, 0)
        flatten(forces[k], flat, g, 3)
        acc = None
        for start, width in CHUNKS:
            for t in range(start, start + width, 128):
                at = slice(t, t + 128)
                along_x = hat(flat[g, 0:1, at], 32, 0.0)
                along_z = hat_z(flat[g, 2:3, at])
                y = jnp.broadcast_to(flat[g, 1:2, at], (16, 128))
                for j in range(32):
                    along_y = jnp.maximum(0.0, 1.0 - jnp.abs(y - float(j)))
                    table[g, 16 * j : 16 * j + 16, at] = (along_y * along_z).astype(BF16)
                for c in range(3):
                    lifted[32 * c : 32 * c + 32, at] = (flat[g, 3 + c : 4 + c, at] * along_x).astype(BF16)
            at = slice(start, start + width)
            part = lax.dot_general(
                lifted[:, at], table[g, :, at], (((1,), (1,)), ((), ())), preferred_element_type=F32
            )
            acc = part if acc is None else acc + part
        total[...] += acc

    def sample_group(g, add):
        lane = lax.broadcasted_iota(jnp.int32, (1, 128), 1)
        for start, width in CHUNKS:
            at = slice(start, start + width)
            picked = jnp.dot(velocity[...], table[g, :, at], preferred_element_type=F32)
            along_x = hat(flat[g, 0:1, at], 32, 0.0)
            for c in range(3):
                flat[g, 3 + c : 4 + c, at] = jnp.sum(
                    picked[32 * c : 32 * c + 32] * along_x, axis=0, keepdims=True
                )
        for c in range(3):
            tail = flat[g, 3 + c : 4 + c, MAIN * CAP : LANES]
            for r in range(CAP):
                row = slice(3 * r + c, 3 * r + c + 1)
                step = flat[g, 3 + c : 4 + c, MAIN * r : MAIN * r + MAIN]
                end = tail if r == 0 else pltpu.roll(tail, 128 - 2 * r, 1)
                end = jnp.where(lane < 2, end, 0.0)
                if add:
                    drift[g, row, 0:MAIN] += step
                    drift[g, row, MAIN:WIDE] += end
                else:
                    drift[g, row, 0:MAIN] = step
                    drift[g, row, MAIN:WIDE] = end
                    cells[g, row, 0:MAIN] += step
                    cells[g, row, MAIN:WIDE] += end

    def collide(from_ref):
        def rows(i, _):
            at_x = pl.ds(pl.multiple_of(8 * i, 8), 8)
            for t in range(0, 512, 128):
                at = slice(t, t + 128)
                f = [from_ref[q, at_x, at] for q in range(19)]
                push = [
                    PUSH_SCALE * total[pl.ds(pl.multiple_of(32 * c + 8 * i, 8), 8), at]
                    for c in range(3)
                ]
                density, momentum = moments(f)
                inverse = 1.0 / density
                u = [(momentum[c] + 0.5 * push[c]) * inverse for c in range(3)]
                square = u[0] * u[0] + u[1] * u[1] + u[2] * u[2]
                dot = u[0] * push[0] + u[1] * push[1] + u[2] * push[2]
                rate = RELAX_RATE * density
                half = 1.0 - 0.5 * RELAX_RATE
                base = rate * (1.0 - 1.5 * square) - (3.0 * half) * dot
                for q in range(19):
                    value = base
                    if q:
                        a = signed_sum([(VELOCITY[q][c], u[c]) for c in range(3)])
                        p = signed_sum([(VELOCITY[q][c], push[c]) for c in range(3)])
                        value = base + rate * a * (3.0 + 4.5 * a) + (half * p) * (3.0 + 9.0 * a)
                    post[q, at_x, at] = (1.0 - RELAX_RATE) * f[q] + WEIGHT[q] * value
            return 0

        lax.fori_loop(0, 4, rows, 0)

    def halo_copies(step):
        ends = (
            [(x_send, x_recv, side, (1, 0) if side == 0 else (-1, 0)) for side in range(2)]
            + [(y_send, y_recv, side, (0, 1) if side == 0 else (0, -1)) for side in range(2)]
            + [
                (e_send, e_recv, n, VELOCITY[EDGE_MOVERS[n][0]][:2])
                for n in range(4)
            ]
        )
        return [
            pltpu.make_async_remote_copy(
                src_ref=out.at[step, n],
                dst_ref=into.at[step, n],
                send_sem=halo_send_sem.at[8 * step + k],
                recv_sem=halo_recv_sem.at[8 * step + k],
                device_id=away(dx, dy),
                device_id_type=MESH,
            )
            for k, (out, into, n, (dx, dy)) in enumerate(ends)
        ]

    def exchange(step):
        lane = lax.broadcasted_iota(jnp.int32, (32, 128), 1)
        for n, (q, row, column) in enumerate(EDGE_MOVERS):
            e_send[step, n] = post[q, row : row + 8, column : column + 128]
        for side, (movers, row) in enumerate(((RIGHT_MOVERS, 31), (LEFT_MOVERS, 0))):
            x_send[step, side] = jnp.zeros((8, 512), F32)
            for n, q in enumerate(movers):
                x_send[step, side, n : n + 1, :] = post[q, row : row + 1, :]
        for side, (movers, column, turn) in enumerate(
            ((UPWARD_MOVERS, 384, 16), (DOWNWARD_MOVERS, 0, 0))
        ):
            face = jnp.zeros((32, 128), F32)
            for n, q in enumerate(movers):
                value = post[q, :, column : column + 128]
                shift = (16 * n + turn) % 128
                if shift:
                    value = pltpu.roll(value, shift, 1)
                face = jnp.where((lane >= 16 * n) & (lane < 16 * n + 16), value, face)
            y_send[step, side] = face
        copies = halo_copies(step)
        for copy in copies:
            copy.start()
        for copy in copies:
            copy.wait()

    def shift_rows(value, dx, edge):
        row = lax.broadcasted_iota(jnp.int32, value.shape, 0)
        if dx > 0:
            return jnp.where(row == 0, edge, pltpu.roll(value, 1, 0))
        return jnp.where(row == 31, edge, pltpu.roll(value, 31, 0))

    def stream(step):
        lane = lax.broadcasted_iota(jnp.int32, (32, 128), 1)
        layer = lax.broadcasted_iota(jnp.int32, (32, 512), 1) % CZ
        for q in range(19):
            dx, dy, dz = VELOCITY[q]
            value = post[q]
            if dx:
                side = 0 if dx > 0 else 1
                n = (RIGHT_MOVERS, LEFT_MOVERS)[side].index(q)
                value = shift_rows(value, dx, x_recv[step, side, n : n + 1, :])
            if dy:
                side = 0 if dy > 0 else 1
                n = (UPWARD_MOVERS, DOWNWARD_MOVERS)[side].index(q)
                rim = y_recv[step, side]
                turn = (128 - 16 * n) % 128 if dy > 0 else 112 - 16 * n
                if turn:
                    rim = pltpu.roll(rim, turn, 1)
                if dx:
                    at = [m[0] for m in EDGE_MOVERS].index(q)
                    row = 7 if dx > 0 else 0
                    edge = pltpu.roll(e_recv[step, at], 16 if dy > 0 else 112, 1)
                    rim = shift_rows(rim, dx, edge[row : row + 1, :])
                if dy > 0:
                    value = pltpu.roll(value, CZ, 1)
                    value = jnp.concatenate(
                        [jnp.where(lane < CZ, rim, value[:, 0:128]), value[:, 128:512]], axis=1
                    )
                else:
                    value = pltpu.roll(value, 512 - CZ, 1)
                    value = jnp.concatenate(
                        [value[:, 0:384], jnp.where(lane >= 112, rim, value[:, 384:512])], axis=1
                    )
            if dz > 0:
                value = jnp.where(layer == 0, pltpu.roll(value, CZ - 1 + 512 - 2 * (CZ - 1), 1), pltpu.roll(value, 1, 1))
            if dz < 0:
                value = jnp.where(layer == CZ - 1, pltpu.roll(value, CZ - 1, 1), pltpu.roll(value, 511, 1))
            pops_out[q] = value

        def rows(i, _):
            at_x = pl.ds(pl.multiple_of(16 * i, 16), 16)
            for t in range(0, 512, 128):
                at = slice(t, t + 128)
                density, momentum = moments([pops_out[q, at_x, at] for q in range(19)])
                inverse = 1.0 / density
                for c in range(3):
                    rows_c = pl.ds(pl.multiple_of(32 * c + 16 * i, 16), 16)
                    push = PUSH_SCALE * total[rows_c, at]
                    velocity[rows_c, at] = ((momentum[c] + 0.5 * push) * inverse).astype(BF16)
            return 0

        lax.fori_loop(0, 2, rows, 0)

    for step in range(STEPS):
        total[...] = jnp.zeros_like(total)
        for b in (1, 0, 2):
            if step == 0:
                for g in range(4 * b, 4 * b + 4):
                    if g != SELF:
                        cell_copy(g).wait_recv()
            batch_force(b)

            def one_spread(k, _):
                spread_group(b, k)
                return 0

            lax.fori_loop(0, 4, one_spread, 0)
        collide(pops_ref if step == 0 else pops_out)
        exchange(step)
        stream(step)
        if step < STEPS - 1:

            def one_sample(g, _):
                sample_group(g, False)
                return 0

            lax.fori_loop(0, GROUPS, one_sample, 0)
        else:
            density_out[...] = total[...].reshape(density_out.shape)

            def last_sample(i, _):
                g = lax.rem(i + SELF + 1, GROUPS)
                sample_group(g, True)
                back_copy(g).start()
                return 0

            lax.fori_loop(0, GROUPS - 1, last_sample, 0)
            sample_group(SELF, True)
            returned[SELF] = drift[SELF]

    for g in range(GROUPS):
        if g != SELF:
            back_copy(g).wait_recv()
    for n in range(places_ref.shape[0]):
        block = returned[slot_ref[n] // CAP]
        rank = slot_ref[n] % CAP
        value = block[0:3, 0:vertices]
        for r in range(1, CAP):
            value = jnp.where(rank == r, block[3 * r : 3 * r + 3, 0:vertices], value)
        moved_out[n] = value
    for g in range(GROUPS):
        if g != SELF:
            cell_copy(g).wait_send()
            back_copy(g).wait_send()


def local(populations, positions, stiffness, membrane_shape, neighbours, home_tile):
    nx = lax.axis_size("gx")
    ny = lax.axis_size("gy")
    cells = positions.shape[0]
    offset = jnp.mod(home_tile // ny - lax.axis_index("gx") + 1, nx)
    turn = jnp.mod(home_tile % ny - lax.axis_index("gy"), ny)
    order = jnp.arange(cells, dtype=jnp.int32)
    earlier = (home_tile[:, None] == home_tile[None, :]) & (order[None, :] < order[:, None])
    rank = jnp.sum(earlier.astype(jnp.int32), axis=1)
    slot = (offset * 4 + turn) * CAP + rank
    hit = slot[None, :] == jnp.arange(GROUPS * CAP, dtype=jnp.int32)[:, None]
    source = jnp.sum(jnp.where(hit, order[None, :], 0), axis=1)
    slot_stiffness = jnp.sum(jnp.where(hit, stiffness[None, :], 0.0), axis=1)
    near = jnp.pad(neighbours.T, ((0, 2), (0, WIDE - neighbours.shape[0])), constant_values=-1)
    width_x, plane = populations.shape[1:]
    smem = pl.BlockSpec(memory_space=pltpu.SMEM)
    vmem = pl.BlockSpec(memory_space=pltpu.VMEM)
    return pl.pallas_call(
        functools.partial(kernel, nx, ny),
        out_shape=(
            jax.ShapeDtypeStruct(populations.shape, F32),
            jax.ShapeDtypeStruct(positions.shape, F32),
            jax.ShapeDtypeStruct((3, width_x, plane), F32),
        ),
        in_specs=[smem] * 3 + [vmem] * 4,
        out_specs=(vmem, vmem, vmem),
        scratch_shapes=[
            pltpu.VMEM((GROUPS, 16, WIDE), F32),
            pltpu.VMEM((GROUPS, 16, WIDE), F32),
            pltpu.VMEM((GROUPS, 16, WIDE), F32),
            pltpu.VMEM((GROUPS, 16, WIDE), F32),
            pltpu.VMEM((WIDE, WIDE), F32),
            pltpu.VMEM((WIDE, WIDE), BF16),
            pltpu.VMEM((1, WIDE), F32),
            pltpu.VMEM((16, WIDE), F32),
            pltpu.VMEM((4, 16, WIDE), F32),
            pltpu.VMEM((GROUPS, 8, LANES), F32),
            pltpu.VMEM((GROUPS, plane, LANES), BF16),
            pltpu.VMEM((3 * width_x, LANES), BF16),
            pltpu.VMEM((3 * width_x, plane), F32),
            pltpu.VMEM(populations.shape, F32),
            pltpu.VMEM((3 * width_x, plane), BF16),
            pltpu.VMEM((STEPS, 2, 8, plane), F32),
            pltpu.VMEM((STEPS, 2, width_x, 128), F32),
            pltpu.VMEM((STEPS, 4, 8, 128), F32),
            pltpu.VMEM((STEPS, 2, 8, plane), F32),
            pltpu.VMEM((STEPS, 2, width_x, 128), F32),
            pltpu.VMEM((STEPS, 4, 8, 128), F32),
            pltpu.SemaphoreType.DMA((GROUPS,)),
            pltpu.SemaphoreType.DMA((GROUPS,)),
            pltpu.SemaphoreType.DMA((GROUPS,)),
            pltpu.SemaphoreType.DMA((GROUPS,)),
            pltpu.SemaphoreType.DMA((8 * STEPS,)),
            pltpu.SemaphoreType.DMA((8 * STEPS,)),
        ],
        compiler_params=pltpu.CompilerParams(
            collective_id=0, has_side_effects=True, vmem_limit_bytes=58 * 2**20
        ),
    )(source, slot_stiffness, slot, populations, positions, membrane_shape, near)


def solution(mesh):
    placed = (
        P(None, "gx", "gy"),
        P(("gx", "gy"), None, None),
        P(("gx", "gy")),
        P(),
        P(),
        P(("gx", "gy")),
    )
    return jax.shard_map(
        local,
        mesh=mesh,
        in_specs=placed,
        out_specs=(P(None, "gx", "gy"), P(("gx", "gy"), None, None), P(None, "gx", "gy")),
        check_vma=False,
    )
```

```python
import functools

import jax
import jax.numpy as jnp
from jax import lax
from jax.experimental import pallas as pl
from jax.experimental.pallas import tpu as pltpu
from jax.sharding import PartitionSpec as P

CZ = 16
CAP = 4
STEPS = 2
GROUPS = 12
SELF = 0
BATCH = 3
WIDE = 768
MAIN = 640
LANES = CAP * MAIN + 128
MESSAGE = 1024
CHUNKS = [(0, 512), (512, 512), (1024, 512), (1536, 512), (2048, 512), (2560, 128)]

VELOCITY = [
    (0, 0, 0),
    (1, 0, 0),
    (-1, 0, 0),
    (0, 1, 0),
    (0, -1, 0),
    (0, 0, 1),
    (0, 0, -1),
    (1, 1, 0),
    (-1, -1, 0),
    (1, -1, 0),
    (-1, 1, 0),
    (1, 0, 1),
    (-1, 0, -1),
    (1, 0, -1),
    (-1, 0, 1),
    (0, 1, 1),
    (0, -1, -1),
    (0, 1, -1),
    (0, -1, 1),
]
WEIGHT = [1.0 / 3.0] + [1.0 / 18.0] * 6 + [1.0 / 36.0] * 12
RIGHT_MOVERS = [1, 7, 9, 11, 13]
LEFT_MOVERS = [2, 8, 10, 12, 14]
UPWARD_MOVERS = [3, 7, 10, 15, 17]
DOWNWARD_MOVERS = [4, 8, 9, 16, 18]
EDGE_MOVERS = [(7, 24, 384), (8, 0, 0), (9, 24, 0), (10, 0, 384)]
RELAX_RATE = 1.25
PUSH_SCALE = 0.05
TETHER_GAIN = 2.0
MESH = pl.DeviceIdType.MESH
F32 = jnp.float32
BF16 = jnp.bfloat16


def signed_sum(parts):
    total = None
    for sign, value in parts:
        if sign == 0:
            continue
        if total is None:
            total = value if sign > 0 else -value
        else:
            total = total + value if sign > 0 else total - value
    return total


def moments(f):
    density = f[0]
    for q in range(1, 19):
        density = density + f[q]
    momentum = [signed_sum([(VELOCITY[q][c], f[q]) for q in range(1, 19)]) for c in range(3)]
    return density, momentum


def hat(row, count, first):
    grid = lax.broadcasted_iota(jnp.int32, (count, row.shape[1]), 0).astype(F32) + first
    return jnp.maximum(0.0, 1.0 - jnp.abs(row - grid))


def hat_z(row):
    wrapped = row - CZ * jnp.floor(row * (1.0 / CZ))
    grid = lax.broadcasted_iota(jnp.int32, (CZ, row.shape[1]), 0).astype(F32)
    gap = jnp.abs(wrapped - grid)
    return jnp.maximum(0.0, 1.0 - jnp.minimum(gap, CZ - gap))


def cut(value):
    high = value.astype(BF16)
    rest = value - high.astype(F32)
    middle = rest.astype(BF16)
    return high, middle, (rest - middle.astype(F32)).astype(BF16)


def chosen(choice, rows):
    parts = [jnp.dot(choice, part, preferred_element_type=F32) for part in cut(rows)]
    return (parts[0] + parts[1]) + parts[2]


def kernel(
    nx,
    ny,
    pops_ref,
    places_ref,
    stiff_ref,
    home_ref,
    shape_ref,
    near_ref,
    pops_out,
    moved_out,
    density_out,
    sendbuf,
    received,
    backbuf,
    returned,
    cells,
    drift,
    gathered,
    tails,
    cell_rows,
    places_pad,
    near,
    matrix32,
    matrix,
    diagonal,
    shapes,
    forces,
    flat,
    table,
    lifted,
    total,
    turned,
    pops,
    post,
    velocity,
    x_send,
    y_send,
    e_send,
    x_recv,
    y_recv,
    e_recv,
    cell_send_sem,
    cell_recv_sem,
    back_send_sem,
    back_recv_sem,
    halo_send_sem,
    halo_recv_sem,
    local_sem,
):
    load = pltpu.make_async_copy(pops_ref, pops, local_sem.at[0])
    load.start()
    me_x = lax.axis_index("gx")
    me_y = lax.axis_index("gy")
    vertices = places_ref.shape[2]
    near[...] = jnp.full((8, WIDE), -1, jnp.int32)
    near[0:6, 0:vertices] = near_ref[...]

    def away(dx, dy):
        return (lax.rem(me_x + dx + nx, nx), lax.rem(me_y + dy + ny, ny))

    barrier = pltpu.get_barrier_semaphore()
    for g in range(GROUPS):
        if g != SELF:
            pl.semaphore_signal(barrier, inc=1, device_id=away((g % 3 + 1) % 3 - 1, g // 3), device_id_type=MESH)

    count = places_ref.shape[1]
    cell_rows[...] = jnp.full((8, 128), -1.0, F32)
    cell_rows[0:1, 0:count] = home_ref[...].astype(F32)
    cell_rows[1:2, 0:count] = stiff_ref[...]
    home = jnp.broadcast_to(cell_rows[0:1, :], (128, 128))
    across = lax.broadcasted_iota(jnp.int32, (128, 128), 1)
    down = lax.broadcasted_iota(jnp.int32, (128, 128), 0)
    earlier = (home == home.T) & (down < across)
    rank = jnp.sum(jnp.where(earlier, 1.0, 0.0), axis=0, keepdims=True)
    home = cell_rows[0:1, :]
    tile_x = jnp.floor((home + 0.5) * (1.0 / ny))
    offset = tile_x - (me_x - 1).astype(F32)
    offset = jnp.where(offset < 0, offset + nx, offset)
    offset = jnp.where(offset >= nx, offset - nx, offset)
    turn = home - ny * tile_x - me_y.astype(F32)
    turn = jnp.where(turn < 0, turn + ny, turn)
    lane = lax.broadcasted_iota(jnp.int32, (1, 128), 1)
    side = jnp.where(offset < 1, offset + 2, offset - 1)
    slot = jnp.where(lane < count, (turn * 3 + side) * CAP + rank, -1.0)
    hit = jnp.where(slot == down.astype(F32), 1.0, 0.0)
    put = hit[0 : GROUPS * CAP, 0:32].astype(BF16)
    take = hit.T[0:32, 0 : GROUPS * CAP].astype(BF16)
    stiff = jnp.sum(hit * cell_rows[1:2, :], axis=1, keepdims=True)[0 : GROUPS * CAP]
    places_pad[...] = jnp.zeros_like(places_pad)
    for c in range(3):
        places_pad[c, 0:count, 0:vertices] = places_ref[c]
        gathered[c] = chosen(put, places_pad[c])
    lanes = lax.broadcasted_iota(jnp.int32, (GROUPS * CAP, 128), 1)
    tails[...] = jnp.where(
        lanes < 2,
        gathered[0, :, MAIN:WIDE],
        jnp.where(
            lanes < 4,
            pltpu.roll(gathered[1, :, MAIN:WIDE], 2, 1),
            jnp.where(lanes < 6, pltpu.roll(gathered[2, :, MAIN:WIDE], 4, 1), stiff),
        ),
    )

    def fold(into, at, rows):
        into[at, 0:4, 0:MAIN] = rows(0, 0, MAIN)
        into[at, 4:8, 0:MAIN] = rows(1, 0, MAIN)
        into[at, 0:4, 640:896] = rows(2, 0, 256)
        into[at, 4:8, 640:896] = rows(2, 256, 512)
        into[at, 0:4, 896:1024] = rows(2, 512, MAIN)

    for g in range(GROUPS):
        into = received if g == SELF else sendbuf
        fold(into, g, lambda c, first, last, g=g: gathered[c, 4 * g : 4 * g + 4, first:last])
        into[g, 4:8, 896:1024] = tails[4 * g : 4 * g + 4, :]
    pl.semaphore_wait(barrier, GROUPS - 1)

    def cell_copy(g):
        return pltpu.make_async_remote_copy(
            src_ref=sendbuf.at[g],
            dst_ref=received.at[g],
            send_sem=cell_send_sem.at[g],
            recv_sem=cell_recv_sem.at[g],
            device_id=away((g % 3 + 1) % 3 - 1, g // 3),
            device_id_type=MESH,
        )

    def back_copy(g):
        return pltpu.make_async_remote_copy(
            src_ref=backbuf.at[g],
            dst_ref=returned.at[g],
            send_sem=back_send_sem.at[g],
            recv_sem=back_recv_sem.at[g],
            device_id=away(1 - (g % 3 + 1) % 3, ny - g // 3),
            device_id_type=MESH,
        )

    for g in (1, 2, 3, 9, 4, 10, 5, 11, 6, 7, 8):
        cell_copy(g).start()

    def link_rows(b, _):
        first = pl.multiple_of(b * 8, 8)
        rows = lax.broadcasted_iota(jnp.int32, (8, WIDE), 0) + first
        count = jnp.zeros((8, WIDE), F32)
        for n in range(6):
            count = count + jnp.where(near[n : n + 1, :] == rows, 1.0, 0.0)
        matrix32[pl.ds(first, 8), :] = count
        return 0

    lax.fori_loop(0, WIDE // 8, link_rows, 0)
    degree = jnp.zeros((1, WIDE), F32)
    for b in range(WIDE // 128):
        both = matrix32[128 * b : 128 * b + 128, :] + matrix32[:, 128 * b : 128 * b + 128].T
        matrix[128 * b : 128 * b + 128, :] = both.astype(BF16)
        degree = degree + jnp.sum(both, axis=0, keepdims=True)
    inside = lax.broadcasted_iota(jnp.int32, (1, WIDE), 1) < vertices
    diagonal[...] = jnp.where(inside, degree + TETHER_GAIN, 0.0)
    shapes[...] = jnp.zeros_like(shapes)
    for c in range(3):
        shapes[4 * c : 4 * c + 4, 0:vertices] = jnp.broadcast_to(shape_ref[c : c + 1, :], (4, vertices))

    def unfold(from_ref, g, put_rows):
        put_rows(0, 0, MAIN, from_ref[g, 0:4, 0:MAIN])
        put_rows(1, 0, MAIN, from_ref[g, 4:8, 0:MAIN])
        put_rows(2, 0, 256, from_ref[g, 0:4, 640:896])
        put_rows(2, 256, 512, from_ref[g, 4:8, 640:896])
        put_rows(2, 512, MAIN, from_ref[g, 0:4, 896:1024])

    def arrive(g):
        def put_rows(c, first, last, value):
            cells[g, 4 * c : 4 * c + 4, first:last] = value

        unfold(received, g, put_rows)
        tail = received[g, 4:8, 896:1024]
        stiff = jnp.broadcast_to(tail[:, 6:7], (4, 128))
        lanes = lax.broadcasted_iota(jnp.int32, (4, 128), 1)
        for c in range(3):
            end = pltpu.roll(tail, 128 - 2 * c, 1) if c else tail
            cells[g, 4 * c : 4 * c + 4, MAIN:WIDE] = jnp.where(lanes < 2, end, stiff)
        cells[g, 12:16, :] = jnp.zeros((4, WIDE), F32)

    def batch_force(b):
        x = cells[BATCH * b : BATCH * b + BATCH].reshape(16 * BATCH, WIDE)
        keep = lax.broadcasted_iota(jnp.int32, (16 * BATCH, WIDE), 1) < vertices
        center = jnp.sum(jnp.where(keep, x, 0.0), axis=1, keepdims=True) * (1.0 / vertices)
        shape = jnp.concatenate([shapes[...]] * BATCH, axis=0)
        strain = jnp.where(keep, x - center - shape, 0.0)
        parts = jnp.dot(
            jnp.concatenate(cut(strain), axis=0), matrix[...], preferred_element_type=F32
        )
        linked = parts[0:48] + parts[48:96] + parts[96:144]
        pulled = strain * diagonal[...] - linked
        forces[...] = (-x[:, vertices : vertices + 1] * pulled).reshape(BATCH, 16, WIDE)

    def flatten(block, into, g, row):
        lane = lax.broadcasted_iota(jnp.int32, (1, 128), 1)
        for c in range(3):
            tail = jnp.zeros((1, 128), F32)
            for r in range(CAP):
                into[g, row + c : row + c + 1, MAIN * r : MAIN * r + MAIN] = block[
                    4 * c + r : 4 * c + r + 1, 0:MAIN
                ]
                end = block[4 * c + r : 4 * c + r + 1, MAIN:WIDE]
                if r:
                    end = pltpu.roll(end, 2 * r, 1)
                tail = jnp.where((lane >= 2 * r) & (lane < 2 * r + 2), end, tail)
            into[g, row + c : row + c + 1, MAIN * CAP : LANES] = tail

    def spread_group(b, k):
        g = BATCH * b + k
        flatten(cells[g], flat, g, 0)
        flatten(forces[k], flat, g, 3)
        for t in range(0, LANES, 128):
            at = slice(t, t + 128)
            along_x = hat(flat[g, 0:1, at], 32, 0.0)
            along_y = hat(flat[g, 1:2, at], 32, 0.0)
            along_z = hat_z(flat[g, 2:3, at])
            for j in range(32):
                table[g, 16 * j : 16 * j + 16, at] = (along_y[j : j + 1] * along_z).astype(BF16)
            for c in range(3):
                lifted[32 * c : 32 * c + 32, at] = (flat[g, 3 + c : 4 + c, at] * along_x).astype(BF16)
        turned[...] += lax.dot_general(
            table[g], lifted[...], (((1,), (1,)), ((), ())), preferred_element_type=F32
        )

    def sample_group(g, add):
        lane = lax.broadcasted_iota(jnp.int32, (1, 128), 1)
        for start, width in CHUNKS:
            at = slice(start, start + width)
            picked = jnp.dot(velocity[...], table[g, :, at], preferred_element_type=F32)
            along_x = hat(flat[g, 0:1, at], 32, 0.0)
            for c in range(3):
                flat[g, 3 + c : 4 + c, at] = jnp.sum(
                    picked[32 * c : 32 * c + 32] * along_x, axis=0, keepdims=True
                )
        for c in range(3):
            tail = flat[g, 3 + c : 4 + c, MAIN * CAP : LANES]
            for r in range(CAP):
                row = slice(4 * c + r, 4 * c + r + 1)
                step = flat[g, 3 + c : 4 + c, MAIN * r : MAIN * r + MAIN]
                end = tail if r == 0 else pltpu.roll(tail, 128 - 2 * r, 1)
                end = jnp.where(lane < 2, end, 0.0)
                if add:
                    drift[g, row, 0:MAIN] += step
                    drift[g, row, MAIN:WIDE] += end
                else:
                    drift[g, row, 0:MAIN] = step
                    drift[g, row, MAIN:WIDE] = end
                    cells[g, row, 0:MAIN] += step
                    cells[g, row, MAIN:WIDE] += end

    def give_back(into, g):
        fold(into, g, lambda c, first, last: drift[g, 4 * c : 4 * c + 4, first:last])
        lanes = lax.broadcasted_iota(jnp.int32, (4, 128), 1)
        ends = [drift[g, 4 * c : 4 * c + 4, MAIN:WIDE] for c in range(3)]
        into[g, 4:8, 896:1024] = jnp.where(
            lanes < 2, ends[0], jnp.where(lanes < 4, pltpu.roll(ends[1], 2, 1), pltpu.roll(ends[2], 4, 1))
        )

    def collide(from_ref):
        def rows(i, _):
            at_x = pl.ds(pl.multiple_of(8 * i, 8), 8)
            for t in range(0, 512, 128):
                at = slice(t, t + 128)
                f = [from_ref[q, at_x, at] for q in range(19)]
                push = [
                    PUSH_SCALE * total[pl.ds(pl.multiple_of(32 * c + 8 * i, 8), 8), at]
                    for c in range(3)
                ]
                density, momentum = moments(f)
                inverse = 1.0 / density
                u = [(momentum[c] + 0.5 * push[c]) * inverse for c in range(3)]
                square = u[0] * u[0] + u[1] * u[1] + u[2] * u[2]
                dot = u[0] * push[0] + u[1] * push[1] + u[2] * push[2]
                rate = RELAX_RATE * density
                half = 1.0 - 0.5 * RELAX_RATE
                base = rate * (1.0 - 1.5 * square) - (3.0 * half) * dot
                for q in range(19):
                    value = base
                    if q:
                        a = signed_sum([(VELOCITY[q][c], u[c]) for c in range(3)])
                        p = signed_sum([(VELOCITY[q][c], push[c]) for c in range(3)])
                        value = base + rate * a * (3.0 + 4.5 * a) + (half * p) * (3.0 + 9.0 * a)
                    post[q, at_x, at] = (1.0 - RELAX_RATE) * f[q] + WEIGHT[q] * value
            return 0

        lax.fori_loop(0, 4, rows, 0)

    def halo_copies(step):
        ends = (
            [(x_send, x_recv, side, (1, 0) if side == 0 else (-1, 0)) for side in range(2)]
            + [(y_send, y_recv, side, (0, 1) if side == 0 else (0, -1)) for side in range(2)]
            + [
                (e_send, e_recv, n, VELOCITY[EDGE_MOVERS[n][0]][:2])
                for n in range(4)
            ]
        )
        return [
            pltpu.make_async_remote_copy(
                src_ref=out.at[step, n],
                dst_ref=into.at[step, n],
                send_sem=halo_send_sem.at[8 * step + k],
                recv_sem=halo_recv_sem.at[8 * step + k],
                device_id=away(dx, dy),
                device_id_type=MESH,
            )
            for k, (out, into, n, (dx, dy)) in enumerate(ends)
        ]

    def exchange(step):
        lane = lax.broadcasted_iota(jnp.int32, (32, 128), 1)
        for n, (q, row, column) in enumerate(EDGE_MOVERS):
            e_send[step, n] = post[q, row : row + 8, column : column + 128]
        for side, (movers, row) in enumerate(((RIGHT_MOVERS, 31), (LEFT_MOVERS, 0))):
            x_send[step, side] = jnp.zeros((8, 512), F32)
            for n, q in enumerate(movers):
                x_send[step, side, n : n + 1, :] = post[q, row : row + 1, :]
        for side, (movers, column, turn) in enumerate(
            ((UPWARD_MOVERS, 384, 16), (DOWNWARD_MOVERS, 0, 0))
        ):
            face = jnp.zeros((32, 128), F32)
            for n, q in enumerate(movers):
                value = post[q, :, column : column + 128]
                shift = (16 * n + turn) % 128
                if shift:
                    value = pltpu.roll(value, shift, 1)
                face = jnp.where((lane >= 16 * n) & (lane < 16 * n + 16), value, face)
            y_send[step, side] = face
        copies = halo_copies(step)
        for copy in copies:
            copy.start()
        for copy in copies:
            copy.wait()

    def shift_rows(value, dx, edge):
        row = lax.broadcasted_iota(jnp.int32, value.shape, 0)
        if dx > 0:
            return jnp.where(row == 0, edge, pltpu.roll(value, 1, 0))
        return jnp.where(row == 31, edge, pltpu.roll(value, 31, 0))

    def stream(step):
        lane = lax.broadcasted_iota(jnp.int32, (32, 128), 1)
        layer = lax.broadcasted_iota(jnp.int32, (32, 512), 1) % CZ
        for q in range(19):
            dx, dy, dz = VELOCITY[q]
            value = post[q]
            if dx:
                side = 0 if dx > 0 else 1
                n = (RIGHT_MOVERS, LEFT_MOVERS)[side].index(q)
                value = shift_rows(value, dx, x_recv[step, side, n : n + 1, :])
            if dy:
                side = 0 if dy > 0 else 1
                n = (UPWARD_MOVERS, DOWNWARD_MOVERS)[side].index(q)
                rim = y_recv[step, side]
                turn = (128 - 16 * n) % 128 if dy > 0 else 112 - 16 * n
                if turn:
                    rim = pltpu.roll(rim, turn, 1)
                if dx:
                    at = [m[0] for m in EDGE_MOVERS].index(q)
                    row = 7 if dx > 0 else 0
                    edge = pltpu.roll(e_recv[step, at], 16 if dy > 0 else 112, 1)
                    rim = shift_rows(rim, dx, edge[row : row + 1, :])
                if dy > 0:
                    value = pltpu.roll(value, CZ, 1)
                    value = jnp.concatenate(
                        [jnp.where(lane < CZ, rim, value[:, 0:128]), value[:, 128:512]], axis=1
                    )
                else:
                    value = pltpu.roll(value, 512 - CZ, 1)
                    value = jnp.concatenate(
                        [value[:, 0:384], jnp.where(lane >= 112, rim, value[:, 384:512])], axis=1
                    )
            if dz > 0:
                value = jnp.where(layer == 0, pltpu.roll(value, CZ - 1 + 512 - 2 * (CZ - 1), 1), pltpu.roll(value, 1, 1))
            if dz < 0:
                value = jnp.where(layer == CZ - 1, pltpu.roll(value, CZ - 1, 1), pltpu.roll(value, 511, 1))
            pops[q] = value

        def rows(i, _):
            at_x = pl.ds(pl.multiple_of(16 * i, 16), 16)
            for t in range(0, 512, 128):
                at = slice(t, t + 128)
                density, momentum = moments([pops[q, at_x, at] for q in range(19)])
                inverse = 1.0 / density
                for c in range(3):
                    rows_c = pl.ds(pl.multiple_of(32 * c + 16 * i, 16), 16)
                    push = PUSH_SCALE * total[rows_c, at]
                    velocity[rows_c, at] = ((momentum[c] + 0.5 * push) * inverse).astype(BF16)
            return 0

        lax.fori_loop(0, 2, rows, 0)

    for step in range(STEPS):
        turned[...] = jnp.zeros_like(turned)
        for b in (0, 1, 3, 2):
            if step == 0:
                for g in range(BATCH * b, BATCH * b + BATCH):
                    if g != SELF:
                        cell_copy(g).wait_recv()
                    arrive(g)
            batch_force(b)

            def one_spread(k, _):
                spread_group(b, k)
                return 0

            lax.fori_loop(0, BATCH, one_spread, 0)
        total[...] = turned[...].T
        if step == 0:
            load.wait()
        collide(pops)
        exchange(step)
        stream(step)
        if step < STEPS - 1:

            def one_sample(g, _):
                sample_group(g, False)
                return 0

            lax.fori_loop(0, GROUPS, one_sample, 0)
        else:
            store_pops = pltpu.make_async_copy(pops, pops_out, local_sem.at[1])
            store_pops.start()
            stores = [
                pltpu.make_async_copy(total.at[32 * c : 32 * c + 32], density_out.at[c], local_sem.at[2 + c])
                for c in range(3)
            ]
            for store in stores:
                store.start()

            def last_sample(i, _):
                g = GROUPS - 1 - i
                sample_group(g, True)
                give_back(backbuf, g)
                back_copy(g).start()
                return 0

            lax.fori_loop(0, GROUPS - 1, last_sample, 0)
            sample_group(SELF, True)
            give_back(returned, SELF)

    for g in range(GROUPS):
        if g != SELF:
            back_copy(g).wait_recv()
    for g in range(GROUPS):

        def put_rows(c, first, last, value):
            gathered[c, 4 * g : 4 * g + 4, first:last] = value

        unfold(returned, g, put_rows)
        tails[4 * g : 4 * g + 4, :] = returned[g, 4:8, 896:1024]
    for c in range(3):
        tail = tails[...]
        gathered[c, :, MAIN:WIDE] = pltpu.roll(tail, 128 - 2 * c, 1) if c else tail
        moved_out[c] = chosen(take, gathered[c])[0:count, 0:vertices]
    store_pops.wait()
    for store in stores:
        store.wait()
    for g in range(GROUPS):
        if g != SELF:
            cell_copy(g).wait_send()
            back_copy(g).wait_send()


def hand_out(a, b, c, a_out, b_out, c_out, a_held, b_held, c_held, in_sems, out_sems):
    pieces = [(a, a_held, a_out, slice(q, min(q + 4, 19))) for q in range(0, 19, 4)]
    pieces += [(b, b_held, b_out, slice(0, 3)), (c, c_held, c_out, slice(0, 3))]
    loads = [
        pltpu.make_async_copy(source.at[at], held.at[at], in_sems.at[n])
        for n, (source, held, _, at) in enumerate(pieces)
    ]
    stores = [
        pltpu.make_async_copy(held.at[at], target.at[at], out_sems.at[n])
        for n, (_, held, target, at) in enumerate(pieces)
    ]
    for load in loads:
        load.start()
    for load, store in zip(loads, stores, strict=True):
        load.wait()
        store.start()
    for store in stores:
        store.wait()


def local(populations, positions, stiffness, membrane_shape, neighbours, home_tile):
    nx = lax.axis_size("gx")
    ny = lax.axis_size("gy")
    places = positions.transpose(1, 0, 2)
    width_x, plane = populations.shape[1:]
    vmem = pl.BlockSpec(memory_space=pltpu.VMEM)
    hbm = pl.BlockSpec(memory_space=pl.ANY)
    populations, moved, density = pl.pallas_call(
        functools.partial(kernel, nx, ny),
        out_shape=(
            jax.ShapeDtypeStruct(populations.shape, F32),
            jax.ShapeDtypeStruct(places.shape, F32),
            jax.ShapeDtypeStruct((3, width_x, plane), F32),
        ),
        in_specs=[hbm] + [vmem] * 5,
        out_specs=(hbm, vmem, hbm),
        scratch_shapes=[
            pltpu.VMEM((GROUPS, 8, MESSAGE), F32),
            pltpu.VMEM((GROUPS, 8, MESSAGE), F32),
            pltpu.VMEM((GROUPS, 8, MESSAGE), F32),
            pltpu.VMEM((GROUPS, 8, MESSAGE), F32),
            pltpu.VMEM((GROUPS, 16, WIDE), F32),
            pltpu.VMEM((GROUPS, 16, WIDE), F32),
            pltpu.VMEM((3, GROUPS * CAP, WIDE), F32),
            pltpu.VMEM((GROUPS * CAP, 128), F32),
            pltpu.VMEM((8, 128), F32),
            pltpu.VMEM((3, 32, WIDE), F32),
            pltpu.VMEM((8, WIDE), jnp.int32),
            pltpu.VMEM((WIDE, WIDE), F32),
            pltpu.VMEM((WIDE, WIDE), BF16),
            pltpu.VMEM((1, WIDE), F32),
            pltpu.VMEM((16, WIDE), F32),
            pltpu.VMEM((BATCH, 16, WIDE), F32),
            pltpu.VMEM((GROUPS, 8, LANES), F32),
            pltpu.VMEM((GROUPS, plane, LANES), BF16),
            pltpu.VMEM((3 * width_x, LANES), BF16),
            pltpu.VMEM((3 * width_x, plane), F32),
            pltpu.VMEM((plane, 3 * width_x), F32),
            pltpu.VMEM(populations.shape, F32),
            pltpu.VMEM(populations.shape, F32),
            pltpu.VMEM((3 * width_x, plane), BF16),
            pltpu.VMEM((STEPS, 2, 8, plane), F32),
            pltpu.VMEM((STEPS, 2, width_x, 128), F32),
            pltpu.VMEM((STEPS, 4, 8, 128), F32),
            pltpu.VMEM((STEPS, 2, 8, plane), F32),
            pltpu.VMEM((STEPS, 2, width_x, 128), F32),
            pltpu.VMEM((STEPS, 4, 8, 128), F32),
            pltpu.SemaphoreType.DMA((GROUPS,)),
            pltpu.SemaphoreType.DMA((GROUPS,)),
            pltpu.SemaphoreType.DMA((GROUPS,)),
            pltpu.SemaphoreType.DMA((GROUPS,)),
            pltpu.SemaphoreType.DMA((8 * STEPS,)),
            pltpu.SemaphoreType.DMA((8 * STEPS,)),
            pltpu.SemaphoreType.DMA((5,)),
        ],
        compiler_params=pltpu.CompilerParams(
            collective_id=0, has_side_effects=True, vmem_limit_bytes=58 * 2**20
        ),
    )(populations, places, stiffness[None], home_tile[None], membrane_shape, neighbours.T)
    results = (populations, moved, density)
    populations, moved, density = pl.pallas_call(
        hand_out,
        out_shape=tuple(jax.ShapeDtypeStruct(r.shape, F32) for r in results),
        in_specs=[hbm] * 3,
        out_specs=(hbm,) * 3,
        scratch_shapes=[pltpu.VMEM(r.shape, F32) for r in results]
        + [pltpu.SemaphoreType.DMA((7,)), pltpu.SemaphoreType.DMA((7,))],
    )(*results)
    return populations, moved.transpose(1, 0, 2), density


def solution(mesh):
    placed = (
        P(None, "gx", "gy"),
        P(("gx", "gy"), None, None),
        P(("gx", "gy")),
        P(),
        P(),
        P(("gx", "gy")),
    )
    return jax.shard_map(
        local,
        mesh=mesh,
        in_specs=placed,
        out_specs=(P(None, "gx", "gy"), P(("gx", "gy"), None, None), P(None, "gx", "gy")),
        check_vma=False,
    )
```

```python
import functools

import jax
import jax.numpy as jnp
from jax import lax
from jax.experimental import pallas as pl
from jax.experimental.pallas import tpu as pltpu
from jax.sharding import PartitionSpec as P

CZ = 16
CAP = 4
STEPS = 2
GROUPS = 12
SELF = 0
BATCHES = [(0, 1), (1, 2), (3, 3), (9, 3), (6, 3)]
WIDE = 768
MAIN = 640
LANES = CAP * MAIN
MESSAGE = 1024
CHUNKS = [(start, 512) for start in range(0, LANES, 512)]

VELOCITY = [
    (0, 0, 0),
    (1, 0, 0),
    (-1, 0, 0),
    (0, 1, 0),
    (0, -1, 0),
    (0, 0, 1),
    (0, 0, -1),
    (1, 1, 0),
    (-1, -1, 0),
    (1, -1, 0),
    (-1, 1, 0),
    (1, 0, 1),
    (-1, 0, -1),
    (1, 0, -1),
    (-1, 0, 1),
    (0, 1, 1),
    (0, -1, -1),
    (0, 1, -1),
    (0, -1, 1),
]
WEIGHT = [1.0 / 3.0] + [1.0 / 18.0] * 6 + [1.0 / 36.0] * 12
RIGHT_MOVERS = [1, 7, 9, 11, 13]
LEFT_MOVERS = [2, 8, 10, 12, 14]
UPWARD_MOVERS = [3, 7, 10, 15, 17]
DOWNWARD_MOVERS = [4, 8, 9, 16, 18]
EDGE_MOVERS = [(7, 24, 384), (8, 0, 0), (9, 24, 0), (10, 0, 384)]
RELAX_RATE = 1.25
PUSH_SCALE = 0.05
TETHER_GAIN = 2.0
MESH = pl.DeviceIdType.MESH
F32 = jnp.float32
BF16 = jnp.bfloat16


def signed_sum(parts):
    total = None
    for sign, value in parts:
        if sign == 0:
            continue
        if total is None:
            total = value if sign > 0 else -value
        else:
            total = total + value if sign > 0 else total - value
    return total


def moments(f):
    density = f[0]
    for q in range(1, 19):
        density = density + f[q]
    momentum = [signed_sum([(VELOCITY[q][c], f[q]) for q in range(1, 19)]) for c in range(3)]
    return density, momentum


def hat(row, count, first):
    grid = lax.broadcasted_iota(jnp.int32, (count, row.shape[1]), 0).astype(F32) + first
    return jnp.maximum(0.0, 1.0 - jnp.abs(row - grid))


def hat_z(row):
    wrapped = row - CZ * jnp.floor(row * (1.0 / CZ))
    grid = lax.broadcasted_iota(jnp.int32, (CZ, row.shape[1]), 0).astype(F32)
    gap = jnp.abs(wrapped - grid)
    return jnp.maximum(0.0, 1.0 - jnp.minimum(gap, CZ - gap))


def cut(value):
    high = value.astype(BF16)
    rest = value - high.astype(F32)
    middle = rest.astype(BF16)
    return high, middle, (rest - middle.astype(F32)).astype(BF16)


def chosen(choice, rows):
    parts = [jnp.dot(choice, part, preferred_element_type=F32) for part in cut(rows)]
    return (parts[0] + parts[1]) + parts[2]


def kernel(
    nx,
    ny,
    pops_ref,
    places_ref,
    stiff_ref,
    home_ref,
    shape_ref,
    near_ref,
    pops_out,
    moved_out,
    density_out,
    sendbuf,
    received,
    backbuf,
    returned,
    cells,
    drift,
    gathered,
    tails,
    cell_rows,
    places_pad,
    near,
    matrix32,
    matrix,
    diagonal,
    shapes,
    forces,
    flat,
    flat_tail,
    table,
    table_tail,
    lifted,
    total,
    turned,
    pops,
    post,
    velocity,
    x_send,
    y_send,
    e_send,
    x_recv,
    y_recv,
    e_recv,
    cell_send_sem,
    cell_recv_sem,
    back_send_sem,
    back_recv_sem,
    halo_send_sem,
    halo_recv_sem,
    local_sem,
):
    load = pltpu.make_async_copy(pops_ref, pops, local_sem.at[0])
    load.start()
    me_x = lax.axis_index("gx")
    me_y = lax.axis_index("gy")
    vertices = places_ref.shape[2]
    near[...] = jnp.full((8, WIDE), -1, jnp.int32)
    near[0:6, 0:vertices] = near_ref[...]

    def away(dx, dy):
        return (lax.rem(me_x + dx + nx, nx), lax.rem(me_y + dy + ny, ny))

    barrier = pltpu.get_barrier_semaphore()
    for g in range(GROUPS):
        if g != SELF:
            pl.semaphore_signal(barrier, inc=1, device_id=away((g % 3 + 1) % 3 - 1, g // 3), device_id_type=MESH)

    count = places_ref.shape[1]
    cell_rows[...] = jnp.full((8, 128), -1.0, F32)
    cell_rows[0:1, 0:count] = home_ref[...].astype(F32)
    cell_rows[1:2, 0:count] = stiff_ref[...]
    home = jnp.broadcast_to(cell_rows[0:1, :], (128, 128))
    across = lax.broadcasted_iota(jnp.int32, (128, 128), 1)
    down = lax.broadcasted_iota(jnp.int32, (128, 128), 0)
    earlier = (home == home.T) & (down < across)
    rank = jnp.sum(jnp.where(earlier, 1.0, 0.0), axis=0, keepdims=True)
    home = cell_rows[0:1, :]
    tile_x = jnp.floor((home + 0.5) * (1.0 / ny))
    offset = tile_x - (me_x - 1).astype(F32)
    offset = jnp.where(offset < 0, offset + nx, offset)
    offset = jnp.where(offset >= nx, offset - nx, offset)
    turn = home - ny * tile_x - me_y.astype(F32)
    turn = jnp.where(turn < 0, turn + ny, turn)
    lane = lax.broadcasted_iota(jnp.int32, (1, 128), 1)
    side = jnp.where(offset < 1, offset + 2, offset - 1)
    slot = jnp.where(lane < count, (turn * 3 + side) * CAP + rank, -1.0)
    hit = jnp.where(slot == down.astype(F32), 1.0, 0.0)
    put = hit[0 : GROUPS * CAP, 0:32].astype(BF16)
    take = hit.T[0:32, 0 : GROUPS * CAP].astype(BF16)
    stiff = jnp.sum(hit * cell_rows[1:2, :], axis=1, keepdims=True)[0 : GROUPS * CAP]
    places_pad[...] = jnp.zeros_like(places_pad)
    for c in range(3):
        places_pad[c, 0:count, 0:vertices] = places_ref[c]
        gathered[c] = chosen(put, places_pad[c])
    lanes = lax.broadcasted_iota(jnp.int32, (GROUPS * CAP, 128), 1)
    tails[...] = jnp.where(
        lanes < 2,
        gathered[0, :, MAIN:WIDE],
        jnp.where(
            lanes < 4,
            pltpu.roll(gathered[1, :, MAIN:WIDE], 2, 1),
            jnp.where(lanes < 6, pltpu.roll(gathered[2, :, MAIN:WIDE], 4, 1), stiff),
        ),
    )

    def fold(into, at, rows):
        into[at, 0:4, 0:MAIN] = rows(0, 0, MAIN)
        into[at, 4:8, 0:MAIN] = rows(1, 0, MAIN)
        into[at, 0:4, 640:896] = rows(2, 0, 256)
        into[at, 4:8, 640:896] = rows(2, 256, 512)
        into[at, 0:4, 896:1024] = rows(2, 512, MAIN)

    for g in range(GROUPS):
        into = received if g == SELF else sendbuf
        fold(into, g, lambda c, first, last, g=g: gathered[c, 4 * g : 4 * g + 4, first:last])
        into[g, 4:8, 896:1024] = tails[4 * g : 4 * g + 4, :]
    pl.semaphore_wait(barrier, GROUPS - 1)

    def cell_copy(g):
        return pltpu.make_async_remote_copy(
            src_ref=sendbuf.at[g],
            dst_ref=received.at[g],
            send_sem=cell_send_sem.at[g],
            recv_sem=cell_recv_sem.at[g],
            device_id=away((g % 3 + 1) % 3 - 1, g // 3),
            device_id_type=MESH,
        )

    def back_copy(g):
        return pltpu.make_async_remote_copy(
            src_ref=backbuf.at[g],
            dst_ref=returned.at[g],
            send_sem=back_send_sem.at[g],
            recv_sem=back_recv_sem.at[g],
            device_id=away(1 - (g % 3 + 1) % 3, ny - g // 3),
            device_id_type=MESH,
        )

    for g in (1, 2, 3, 9, 4, 10, 5, 11, 6, 7, 8):
        cell_copy(g).start()

    def link_rows(b, _):
        first = pl.multiple_of(b * 8, 8)
        rows = lax.broadcasted_iota(jnp.int32, (8, WIDE), 0) + first
        count = jnp.zeros((8, WIDE), F32)
        for n in range(6):
            count = count + jnp.where(near[n : n + 1, :] == rows, 1.0, 0.0)
        matrix32[pl.ds(first, 8), :] = count
        return 0

    lax.fori_loop(0, WIDE // 8, link_rows, 0)
    degree = jnp.zeros((1, WIDE), F32)
    for b in range(WIDE // 128):
        both = matrix32[128 * b : 128 * b + 128, :] + matrix32[:, 128 * b : 128 * b + 128].T
        matrix[128 * b : 128 * b + 128, :] = both.astype(BF16)
        degree = degree + jnp.sum(both, axis=0, keepdims=True)
    inside = lax.broadcasted_iota(jnp.int32, (1, WIDE), 1) < vertices
    diagonal[...] = jnp.where(inside, degree + TETHER_GAIN, 0.0)
    shapes[...] = jnp.zeros_like(shapes)
    flat_tail[...] = jnp.zeros_like(flat_tail)
    for c in range(3):
        shapes[4 * c : 4 * c + 4, 0:vertices] = jnp.broadcast_to(shape_ref[c : c + 1, :], (4, vertices))

    def unfold(from_ref, g, put_rows):
        put_rows(0, 0, MAIN, from_ref[g, 0:4, 0:MAIN])
        put_rows(1, 0, MAIN, from_ref[g, 4:8, 0:MAIN])
        put_rows(2, 0, 256, from_ref[g, 0:4, 640:896])
        put_rows(2, 256, 512, from_ref[g, 4:8, 640:896])
        put_rows(2, 512, MAIN, from_ref[g, 0:4, 896:1024])

    def arrive(g):
        def put_rows(c, first, last, value):
            cells[g, 4 * c : 4 * c + 4, first:last] = value

        unfold(received, g, put_rows)
        tail = received[g, 4:8, 896:1024]
        stiff = jnp.broadcast_to(tail[:, 6:7], (4, 128))
        lanes = lax.broadcasted_iota(jnp.int32, (4, 128), 1)
        for c in range(3):
            end = pltpu.roll(tail, 128 - 2 * c, 1) if c else tail
            cells[g, 4 * c : 4 * c + 4, MAIN:WIDE] = jnp.where(lanes < 2, end, stiff)
        cells[g, 12:16, :] = jnp.zeros((4, WIDE), F32)

    def batch_force(first, many):
        rows = 16 * many
        x = cells[first : first + many].reshape(rows, WIDE)
        keep = lax.broadcasted_iota(jnp.int32, (rows, WIDE), 1) < vertices
        center = jnp.sum(jnp.where(keep, x, 0.0), axis=1, keepdims=True) * (1.0 / vertices)
        shape = jnp.concatenate([shapes[...]] * many, axis=0)
        strain = jnp.where(keep, x - center - shape, 0.0)
        parts = jnp.dot(
            jnp.concatenate(cut(strain), axis=0), matrix[...], preferred_element_type=F32
        )
        linked = parts[0:rows] + parts[rows : 2 * rows] + parts[2 * rows : 3 * rows]
        pulled = strain * diagonal[...] - linked
        forces[first : first + many] = (-x[:, vertices : vertices + 1] * pulled).reshape(many, 16, WIDE)

    def flatten(block, g, row):
        lane = lax.broadcasted_iota(jnp.int32, (1, 128), 1)
        for c in range(3):
            tail = jnp.zeros((1, 128), F32)
            for r in range(CAP):
                flat[g, row + c : row + c + 1, MAIN * r : MAIN * r + MAIN] = block[
                    4 * c + r : 4 * c + r + 1, 0:MAIN
                ]
                end = block[4 * c + r : 4 * c + r + 1, MAIN:WIDE]
                if r:
                    end = pltpu.roll(end, 2 * r, 1)
                tail = jnp.where((lane >= 2 * r) & (lane < 2 * r + 2), end, tail)
            tail = pltpu.roll(tail, 8 * g, 1)
            mine = (lane >= 8 * g) & (lane < 8 * g + 8)
            flat_tail[row + c : row + c + 1, :] = jnp.where(mine, tail, flat_tail[row + c : row + c + 1, :])

    def tabulate(read, put_table, put_lifted, at):
        along_x = hat(read(0, at), 32, 0.0)
        along_y = hat(read(1, at), 32, 0.0)
        along_z = hat_z(read(2, at))
        for j in range(32):
            put_table(j, at, (along_y[j : j + 1] * along_z).astype(BF16))
        for c in range(3):
            put_lifted(c, at, (read(3 + c, at) * along_x).astype(BF16))

    def put_lifted(c, at, value):
        lifted[32 * c : 32 * c + 32, at] = value

    def spread_group(g):
        flatten(cells[g], g, 0)
        flatten(forces[g], g, 3)

        def put_table(j, at, value):
            table[g, 16 * j : 16 * j + 16, at] = value

        for t in range(0, LANES, 128):
            tabulate(lambda n, at: flat[g, n : n + 1, at], put_table, put_lifted, slice(t, t + 128))
        turned[...] += lax.dot_general(
            table[g], lifted[...], (((1,), (1,)), ((), ())), preferred_element_type=F32
        )

    def spread_tail():
        def put_table(j, at, value):
            table_tail[16 * j : 16 * j + 16, at] = value

        at = slice(0, 128)
        tabulate(lambda n, at: flat_tail[n : n + 1, at], put_table, put_lifted, at)
        turned[...] += lax.dot_general(
            table_tail[...], lifted[:, at], (((1,), (1,)), ((), ())), preferred_element_type=F32
        )

    def drifts(picked, row):
        along_x = hat(row, 32, 0.0)
        return [
            jnp.sum(picked[32 * c : 32 * c + 32] * along_x, axis=0, keepdims=True) for c in range(3)
        ]

    def sample_tail():
        picked = jnp.dot(velocity[...], table_tail[...], preferred_element_type=F32)
        used = lax.broadcasted_iota(jnp.int32, (1, 128), 1) < 8 * GROUPS
        for c, value in enumerate(drifts(picked, flat_tail[0:1, :])):
            flat_tail[3 + c : 4 + c, :] = jnp.where(used, value, 0.0)

    def sample_group(g, add):
        lane = lax.broadcasted_iota(jnp.int32, (1, 128), 1)
        for start, width in CHUNKS:
            at = slice(start, start + width)
            picked = jnp.dot(velocity[...], table[g, :, at], preferred_element_type=F32)
            for c, value in enumerate(drifts(picked, flat[g, 0:1, at])):
                flat[g, 3 + c : 4 + c, at] = value
        for c in range(3):
            tail = pltpu.roll(flat_tail[3 + c : 4 + c, :], 128 - 8 * g, 1)
            for r in range(CAP):
                row = slice(4 * c + r, 4 * c + r + 1)
                step = flat[g, 3 + c : 4 + c, MAIN * r : MAIN * r + MAIN]
                end = tail if r == 0 else pltpu.roll(tail, 128 - 2 * r, 1)
                end = jnp.where(lane < 2, end, 0.0)
                if add:
                    drift[g, row, 0:MAIN] += step
                    drift[g, row, MAIN:WIDE] += end
                else:
                    drift[g, row, 0:MAIN] = step
                    drift[g, row, MAIN:WIDE] = end
                    cells[g, row, 0:MAIN] += step
                    cells[g, row, MAIN:WIDE] += end

    def give_back(into, g):
        fold(into, g, lambda c, first, last: drift[g, 4 * c : 4 * c + 4, first:last])
        lanes = lax.broadcasted_iota(jnp.int32, (4, 128), 1)
        ends = [drift[g, 4 * c : 4 * c + 4, MAIN:WIDE] for c in range(3)]
        into[g, 4:8, 896:1024] = jnp.where(
            lanes < 2, ends[0], jnp.where(lanes < 4, pltpu.roll(ends[1], 2, 1), pltpu.roll(ends[2], 4, 1))
        )

    def collide(from_ref):
        def rows(i, _):
            at_x = pl.ds(pl.multiple_of(8 * i, 8), 8)
            for t in range(0, 512, 128):
                at = slice(t, t + 128)
                f = [from_ref[q, at_x, at] for q in range(19)]
                push = [
                    PUSH_SCALE * total[pl.ds(pl.multiple_of(32 * c + 8 * i, 8), 8), at]
                    for c in range(3)
                ]
                density, momentum = moments(f)
                inverse = 1.0 / density
                u = [(momentum[c] + 0.5 * push[c]) * inverse for c in range(3)]
                square = u[0] * u[0] + u[1] * u[1] + u[2] * u[2]
                dot = u[0] * push[0] + u[1] * push[1] + u[2] * push[2]
                rate = RELAX_RATE * density
                half = 1.0 - 0.5 * RELAX_RATE
                base = rate * (1.0 - 1.5 * square) - (3.0 * half) * dot
                for q in range(19):
                    value = base
                    if q:
                        a = signed_sum([(VELOCITY[q][c], u[c]) for c in range(3)])
                        p = signed_sum([(VELOCITY[q][c], push[c]) for c in range(3)])
                        value = base + rate * a * (3.0 + 4.5 * a) + (half * p) * (3.0 + 9.0 * a)
                    post[q, at_x, at] = (1.0 - RELAX_RATE) * f[q] + WEIGHT[q] * value
            return 0

        lax.fori_loop(0, 4, rows, 0)

    def halo_copies(step):
        ends = (
            [(x_send, x_recv, side, (1, 0) if side == 0 else (-1, 0)) for side in range(2)]
            + [(y_send, y_recv, side, (0, 1) if side == 0 else (0, -1)) for side in range(2)]
            + [
                (e_send, e_recv, n, VELOCITY[EDGE_MOVERS[n][0]][:2])
                for n in range(4)
            ]
        )
        return [
            pltpu.make_async_remote_copy(
                src_ref=out.at[step, n],
                dst_ref=into.at[step, n],
                send_sem=halo_send_sem.at[8 * step + k],
                recv_sem=halo_recv_sem.at[8 * step + k],
                device_id=away(dx, dy),
                device_id_type=MESH,
            )
            for k, (out, into, n, (dx, dy)) in enumerate(ends)
        ]

    def exchange(step):
        lane = lax.broadcasted_iota(jnp.int32, (32, 128), 1)
        for n, (q, row, column) in enumerate(EDGE_MOVERS):
            e_send[step, n] = post[q, row : row + 8, column : column + 128]
        for side, (movers, row) in enumerate(((RIGHT_MOVERS, 31), (LEFT_MOVERS, 0))):
            x_send[step, side] = jnp.zeros((8, 512), F32)
            for n, q in enumerate(movers):
                x_send[step, side, n : n + 1, :] = post[q, row : row + 1, :]
        for side, (movers, column, turn) in enumerate(
            ((UPWARD_MOVERS, 384, 16), (DOWNWARD_MOVERS, 0, 0))
        ):
            face = jnp.zeros((32, 128), F32)
            for n, q in enumerate(movers):
                value = post[q, :, column : column + 128]
                shift = (16 * n + turn) % 128
                if shift:
                    value = pltpu.roll(value, shift, 1)
                face = jnp.where((lane >= 16 * n) & (lane < 16 * n + 16), value, face)
            y_send[step, side] = face
        copies = halo_copies(step)
        for copy in copies:
            copy.start()
        return copies

    def shift_rows(value, dx, edge):
        row = lax.broadcasted_iota(jnp.int32, value.shape, 0)
        if dx > 0:
            return jnp.where(row == 0, edge, pltpu.roll(value, 1, 0))
        return jnp.where(row == 31, edge, pltpu.roll(value, 31, 0))

    def shift_layers(value, dz):
        if dz == 0:
            return value
        width = value.shape[1]
        layer = lax.broadcasted_iota(jnp.int32, value.shape, 1) % CZ
        rim, wrap = (0, width + 1 - CZ) if dz > 0 else (CZ - 1, CZ - 1)
        near_by = pltpu.roll(value, 1 if dz > 0 else width - 1, 1)
        return jnp.where(layer == rim, pltpu.roll(value, wrap, 1), near_by)

    def stream(step, copies):
        for q in range(19):
            dx, dy, dz = VELOCITY[q]
            value = post[q]
            if dx:
                value = pltpu.roll(value, 1 if dx > 0 else 31, 0)
            if dy:
                value = pltpu.roll(value, CZ if dy > 0 else 512 - CZ, 1)
            pops[q] = shift_layers(value, dz)
        for copy in copies:
            copy.wait()
        lane = lax.broadcasted_iota(jnp.int32, (32, 128), 1)
        for q in range(19):
            dx, dy, dz = VELOCITY[q]
            if dx:
                side = 0 if dx > 0 else 1
                n = (RIGHT_MOVERS, LEFT_MOVERS)[side].index(q)
                row = 0 if dx > 0 else 31
                edge = x_recv[step, side, n : n + 1, :]
                if dy:
                    edge = pltpu.roll(edge, CZ if dy > 0 else 512 - CZ, 1)
                pops[q, row : row + 1, :] = shift_layers(edge, dz)
            if dy:
                side = 0 if dy > 0 else 1
                n = (UPWARD_MOVERS, DOWNWARD_MOVERS)[side].index(q)
                rim = y_recv[step, side]
                turn = (128 - 16 * n) % 128 if dy > 0 else 112 - 16 * n
                if turn:
                    rim = pltpu.roll(rim, turn, 1)
                if dx:
                    at = [m[0] for m in EDGE_MOVERS].index(q)
                    row = 7 if dx > 0 else 0
                    edge = pltpu.roll(e_recv[step, at], 16 if dy > 0 else 112, 1)
                    rim = shift_rows(rim, dx, edge[row : row + 1, :])
                rim = shift_layers(rim, dz)
                if dy > 0:
                    pops[q, :, 0:128] = jnp.where(lane < CZ, rim, pops[q, :, 0:128])
                else:
                    pops[q, :, 384:512] = jnp.where(lane >= 128 - CZ, rim, pops[q, :, 384:512])

        def rows(i, _):
            at_x = pl.ds(pl.multiple_of(16 * i, 16), 16)
            for t in range(0, 512, 128):
                at = slice(t, t + 128)
                density, momentum = moments([pops[q, at_x, at] for q in range(19)])
                inverse = 1.0 / density
                for c in range(3):
                    rows_c = pl.ds(pl.multiple_of(32 * c + 16 * i, 16), 16)
                    push = PUSH_SCALE * total[rows_c, at]
                    velocity[rows_c, at] = ((momentum[c] + 0.5 * push) * inverse).astype(BF16)
            return 0

        lax.fori_loop(0, 2, rows, 0)

    for step in range(STEPS):
        turned[...] = jnp.zeros_like(turned)
        for first, many in BATCHES if step == 0 else [(0, GROUPS)]:
            if step == 0:
                for g in range(first, first + many):
                    if g != SELF:
                        cell_copy(g).wait_recv()
                    arrive(g)
            batch_force(first, many)

            def one_spread(g, _):
                spread_group(g)
                return 0

            lax.fori_loop(first, first + many, one_spread, 0)
        spread_tail()
        total[...] = turned[...].T
        if step == 0:
            load.wait()
        collide(pops)
        copies = exchange(step)
        stream(step, copies)
        sample_tail()
        if step < STEPS - 1:

            def one_sample(g, _):
                sample_group(g, False)
                return 0

            lax.fori_loop(0, GROUPS, one_sample, 0)
        else:
            store_pops = pltpu.make_async_copy(pops, pops_out, local_sem.at[1])
            store_pops.start()
            stores = [
                pltpu.make_async_copy(total.at[32 * c : 32 * c + 32], density_out.at[c], local_sem.at[2 + c])
                for c in range(3)
            ]
            for store in stores:
                store.start()

            def last_sample(i, _):
                g = GROUPS - 1 - i
                sample_group(g, True)
                give_back(backbuf, g)
                back_copy(g).start()
                return 0

            lax.fori_loop(0, GROUPS - 1, last_sample, 0)
            sample_group(SELF, True)
            give_back(returned, SELF)

    for g in range(GROUPS):
        if g != SELF:
            back_copy(g).wait_recv()
    for g in range(GROUPS):

        def put_rows(c, first, last, value):
            gathered[c, 4 * g : 4 * g + 4, first:last] = value

        unfold(returned, g, put_rows)
        tails[4 * g : 4 * g + 4, :] = returned[g, 4:8, 896:1024]
    for c in range(3):
        tail = tails[...]
        gathered[c, :, MAIN:WIDE] = pltpu.roll(tail, 128 - 2 * c, 1) if c else tail
        moved_out[c] = chosen(take, gathered[c])[0:count, 0:vertices]
    store_pops.wait()
    for store in stores:
        store.wait()
    for g in range(GROUPS):
        if g != SELF:
            cell_copy(g).wait_send()
            back_copy(g).wait_send()


def hand_out(a, b, c, a_out, b_out, c_out, a_held, b_held, c_held, in_sems, out_sems):
    pieces = [(a, a_held, a_out, slice(q, min(q + 4, 19))) for q in range(0, 19, 4)]
    pieces += [(b, b_held, b_out, slice(0, 3)), (c, c_held, c_out, slice(0, 3))]
    loads = [
        pltpu.make_async_copy(source.at[at], held.at[at], in_sems.at[n])
        for n, (source, held, _, at) in enumerate(pieces)
    ]
    stores = [
        pltpu.make_async_copy(held.at[at], target.at[at], out_sems.at[n])
        for n, (_, held, target, at) in enumerate(pieces)
    ]
    for load in loads:
        load.start()
    for load, store in zip(loads, stores, strict=True):
        load.wait()
        store.start()
    for store in stores:
        store.wait()


def local(populations, positions, stiffness, membrane_shape, neighbours, home_tile):
    nx = lax.axis_size("gx")
    ny = lax.axis_size("gy")
    places = positions.transpose(1, 0, 2)
    width_x, plane = populations.shape[1:]
    vmem = pl.BlockSpec(memory_space=pltpu.VMEM)
    hbm = pl.BlockSpec(memory_space=pl.ANY)
    populations, moved, density = pl.pallas_call(
        functools.partial(kernel, nx, ny),
        out_shape=(
            jax.ShapeDtypeStruct(populations.shape, F32),
            jax.ShapeDtypeStruct(places.shape, F32),
            jax.ShapeDtypeStruct((3, width_x, plane), F32),
        ),
        in_specs=[hbm] + [vmem] * 5,
        out_specs=(hbm, vmem, hbm),
        scratch_shapes=[
            pltpu.VMEM((GROUPS, 8, MESSAGE), F32),
            pltpu.VMEM((GROUPS, 8, MESSAGE), F32),
            pltpu.VMEM((GROUPS, 8, MESSAGE), F32),
            pltpu.VMEM((GROUPS, 8, MESSAGE), F32),
            pltpu.VMEM((GROUPS, 16, WIDE), F32),
            pltpu.VMEM((GROUPS, 16, WIDE), F32),
            pltpu.VMEM((3, GROUPS * CAP, WIDE), F32),
            pltpu.VMEM((GROUPS * CAP, 128), F32),
            pltpu.VMEM((8, 128), F32),
            pltpu.VMEM((3, 32, WIDE), F32),
            pltpu.VMEM((8, WIDE), jnp.int32),
            pltpu.VMEM((WIDE, WIDE), F32),
            pltpu.VMEM((WIDE, WIDE), BF16),
            pltpu.VMEM((1, WIDE), F32),
            pltpu.VMEM((16, WIDE), F32),
            pltpu.VMEM((GROUPS, 16, WIDE), F32),
            pltpu.VMEM((GROUPS, 8, LANES), F32),
            pltpu.VMEM((8, 128), F32),
            pltpu.VMEM((GROUPS, plane, LANES), BF16),
            pltpu.VMEM((plane, 128), BF16),
            pltpu.VMEM((3 * width_x, LANES), BF16),
            pltpu.VMEM((3 * width_x, plane), F32),
            pltpu.VMEM((plane, 3 * width_x), F32),
            pltpu.VMEM(populations.shape, F32),
            pltpu.VMEM(populations.shape, F32),
            pltpu.VMEM((3 * width_x, plane), BF16),
            pltpu.VMEM((STEPS, 2, 8, plane), F32),
            pltpu.VMEM((STEPS, 2, width_x, 128), F32),
            pltpu.VMEM((STEPS, 4, 8, 128), F32),
            pltpu.VMEM((STEPS, 2, 8, plane), F32),
            pltpu.VMEM((STEPS, 2, width_x, 128), F32),
            pltpu.VMEM((STEPS, 4, 8, 128), F32),
            pltpu.SemaphoreType.DMA((GROUPS,)),
            pltpu.SemaphoreType.DMA((GROUPS,)),
            pltpu.SemaphoreType.DMA((GROUPS,)),
            pltpu.SemaphoreType.DMA((GROUPS,)),
            pltpu.SemaphoreType.DMA((8 * STEPS,)),
            pltpu.SemaphoreType.DMA((8 * STEPS,)),
            pltpu.SemaphoreType.DMA((5,)),
        ],
        compiler_params=pltpu.CompilerParams(
            collective_id=0, has_side_effects=True, vmem_limit_bytes=58 * 2**20
        ),
    )(populations, places, stiffness[None], home_tile[None], membrane_shape, neighbours.T)
    results = (populations, moved, density)
    populations, moved, density = pl.pallas_call(
        hand_out,
        out_shape=tuple(jax.ShapeDtypeStruct(r.shape, F32) for r in results),
        in_specs=[hbm] * 3,
        out_specs=(hbm,) * 3,
        scratch_shapes=[pltpu.VMEM(r.shape, F32) for r in results]
        + [pltpu.SemaphoreType.DMA((7,)), pltpu.SemaphoreType.DMA((7,))],
    )(*results)
    return populations, moved.transpose(1, 0, 2), density


def solution(mesh):
    placed = (
        P(None, "gx", "gy"),
        P(("gx", "gy"), None, None),
        P(("gx", "gy")),
        P(),
        P(),
        P(("gx", "gy")),
    )
    return jax.shard_map(
        local,
        mesh=mesh,
        in_specs=placed,
        out_specs=(P(None, "gx", "gy"), P(("gx", "gy"), None, None), P(None, "gx", "gy")),
        check_vma=False,
    )
```

```python
import functools

import jax
import jax.numpy as jnp
from jax import lax
from jax.experimental import pallas as pl
from jax.experimental.pallas import tpu as pltpu
from jax.sharding import PartitionSpec as P

CZ = 16
CAP = 4
STEPS = 2
GROUPS = 12
SELF = 0
BATCHES = [(0, 1), (1, 2), (3, 3), (9, 3), (6, 3)]
WIDE = 768
MAIN = 640
LANES = CAP * MAIN
MESSAGE = 1024
HALF = 16
WINDOW = (HALF + 1) * CZ
CHUNKS = [(start, 512) for start in range(0, LANES, 512)]

VELOCITY = [
    (0, 0, 0),
    (1, 0, 0),
    (-1, 0, 0),
    (0, 1, 0),
    (0, -1, 0),
    (0, 0, 1),
    (0, 0, -1),
    (1, 1, 0),
    (-1, -1, 0),
    (1, -1, 0),
    (-1, 1, 0),
    (1, 0, 1),
    (-1, 0, -1),
    (1, 0, -1),
    (-1, 0, 1),
    (0, 1, 1),
    (0, -1, -1),
    (0, 1, -1),
    (0, -1, 1),
]
WEIGHT = [1.0 / 3.0] + [1.0 / 18.0] * 6 + [1.0 / 36.0] * 12
RIGHT_MOVERS = [1, 7, 9, 11, 13]
LEFT_MOVERS = [2, 8, 10, 12, 14]
UPWARD_MOVERS = [3, 7, 10, 15, 17]
DOWNWARD_MOVERS = [4, 8, 9, 16, 18]
EDGE_MOVERS = [(7, 24, 384), (8, 0, 0), (9, 24, 0), (10, 0, 384)]
RELAX_RATE = 1.25
PUSH_SCALE = 0.05
TETHER_GAIN = 2.0
MESH = pl.DeviceIdType.MESH
F32 = jnp.float32
BF16 = jnp.bfloat16


def signed_sum(parts):
    total = None
    for sign, value in parts:
        if sign == 0:
            continue
        if total is None:
            total = value if sign > 0 else -value
        else:
            total = total + value if sign > 0 else total - value
    return total


def moments(f):
    density = f[0]
    for q in range(1, 19):
        density = density + f[q]
    momentum = [signed_sum([(VELOCITY[q][c], f[q]) for q in range(1, 19)]) for c in range(3)]
    return density, momentum


def hat(row, count, first):
    grid = lax.broadcasted_iota(jnp.int32, (count, row.shape[1]), 0).astype(F32) + first
    return jnp.maximum(0.0, 1.0 - jnp.abs(row - grid))


def hat_z(row):
    wrapped = row - CZ * jnp.floor(row * (1.0 / CZ))
    grid = lax.broadcasted_iota(jnp.int32, (CZ, row.shape[1]), 0).astype(F32)
    gap = jnp.abs(wrapped - grid)
    return jnp.maximum(0.0, 1.0 - jnp.minimum(gap, CZ - gap))


def cut(value):
    high = value.astype(BF16)
    rest = value - high.astype(F32)
    middle = rest.astype(BF16)
    return high, middle, (rest - middle.astype(F32)).astype(BF16)


def chosen(choice, rows):
    parts = [jnp.dot(choice, part, preferred_element_type=F32) for part in cut(rows)]
    return (parts[0] + parts[1]) + parts[2]


def kernel(
    nx,
    ny,
    pops_ref,
    places_ref,
    stiff_ref,
    home_ref,
    shape_ref,
    near_ref,
    pops_out,
    moved_out,
    density_out,
    sendbuf,
    received,
    backbuf,
    returned,
    cells,
    drift,
    gathered,
    tails,
    cell_rows,
    places_pad,
    near,
    matrix32,
    matrix,
    diagonal,
    shapes,
    forces,
    flat,
    flat_tail,
    table,
    table_tail,
    window,
    lifted,
    total,
    turned,
    pops,
    post,
    velocity,
    x_send,
    y_send,
    e_send,
    x_recv,
    y_recv,
    e_recv,
    cell_send_sem,
    cell_recv_sem,
    back_send_sem,
    back_recv_sem,
    halo_send_sem,
    halo_recv_sem,
    local_sem,
):
    load = pltpu.make_async_copy(pops_ref, pops, local_sem.at[0])
    load.start()
    me_x = lax.axis_index("gx")
    me_y = lax.axis_index("gy")
    vertices = places_ref.shape[2]
    near[...] = jnp.full((8, WIDE), -1, jnp.int32)
    near[0:6, 0:vertices] = near_ref[...]

    def away(dx, dy):
        return (lax.rem(me_x + dx + nx, nx), lax.rem(me_y + dy + ny, ny))

    barrier = pltpu.get_barrier_semaphore()
    for g in range(GROUPS):
        if g != SELF:
            pl.semaphore_signal(barrier, inc=1, device_id=away((g % 3 + 1) % 3 - 1, g // 3), device_id_type=MESH)

    count = places_ref.shape[1]
    cell_rows[...] = jnp.full((8, 128), -1.0, F32)
    cell_rows[0:1, 0:count] = home_ref[...].astype(F32)
    cell_rows[1:2, 0:count] = stiff_ref[...]
    home = jnp.broadcast_to(cell_rows[0:1, :], (128, 128))
    across = lax.broadcasted_iota(jnp.int32, (128, 128), 1)
    down = lax.broadcasted_iota(jnp.int32, (128, 128), 0)
    earlier = (home == home.T) & (down < across)
    rank = jnp.sum(jnp.where(earlier, 1.0, 0.0), axis=0, keepdims=True)
    home = cell_rows[0:1, :]
    tile_x = jnp.floor((home + 0.5) * (1.0 / ny))
    offset = tile_x - (me_x - 1).astype(F32)
    offset = jnp.where(offset < 0, offset + nx, offset)
    offset = jnp.where(offset >= nx, offset - nx, offset)
    turn = home - ny * tile_x - me_y.astype(F32)
    turn = jnp.where(turn < 0, turn + ny, turn)
    lane = lax.broadcasted_iota(jnp.int32, (1, 128), 1)
    side = jnp.where(offset < 1, offset + 2, offset - 1)
    slot = jnp.where(lane < count, (turn * 3 + side) * CAP + rank, -1.0)
    hit = jnp.where(slot == down.astype(F32), 1.0, 0.0)
    put = hit[0 : GROUPS * CAP, 0:32].astype(BF16)
    take = hit.T[0:32, 0 : GROUPS * CAP].astype(BF16)
    stiff = jnp.sum(hit * cell_rows[1:2, :], axis=1, keepdims=True)[0 : GROUPS * CAP]
    places_pad[...] = jnp.zeros_like(places_pad)
    for c in range(3):
        places_pad[c, 0:count, 0:vertices] = places_ref[c]
        gathered[c] = chosen(put, places_pad[c])
    lanes = lax.broadcasted_iota(jnp.int32, (GROUPS * CAP, 128), 1)
    tails[...] = jnp.where(
        lanes < 2,
        gathered[0, :, MAIN:WIDE],
        jnp.where(
            lanes < 4,
            pltpu.roll(gathered[1, :, MAIN:WIDE], 2, 1),
            jnp.where(lanes < 6, pltpu.roll(gathered[2, :, MAIN:WIDE], 4, 1), stiff),
        ),
    )

    def fold(into, at, rows):
        into[at, 0:4, 0:MAIN] = rows(0, 0, MAIN)
        into[at, 4:8, 0:MAIN] = rows(1, 0, MAIN)
        into[at, 0:4, 640:896] = rows(2, 0, 256)
        into[at, 4:8, 640:896] = rows(2, 256, 512)
        into[at, 0:4, 896:1024] = rows(2, 512, MAIN)

    for g in range(GROUPS):
        into = received if g == SELF else sendbuf
        fold(into, g, lambda c, first, last, g=g: gathered[c, 4 * g : 4 * g + 4, first:last])
        into[g, 4:8, 896:1024] = tails[4 * g : 4 * g + 4, :]
    pl.semaphore_wait(barrier, GROUPS - 1)

    def cell_copy(g):
        return pltpu.make_async_remote_copy(
            src_ref=sendbuf.at[g],
            dst_ref=received.at[g],
            send_sem=cell_send_sem.at[g],
            recv_sem=cell_recv_sem.at[g],
            device_id=away((g % 3 + 1) % 3 - 1, g // 3),
            device_id_type=MESH,
        )

    def back_copy(g):
        return pltpu.make_async_remote_copy(
            src_ref=backbuf.at[g],
            dst_ref=returned.at[g],
            send_sem=back_send_sem.at[g],
            recv_sem=back_recv_sem.at[g],
            device_id=away(1 - (g % 3 + 1) % 3, ny - g // 3),
            device_id_type=MESH,
        )

    for g in (1, 2, 3, 9, 4, 10, 5, 11, 6, 7, 8):
        cell_copy(g).start()

    def link_rows(b, _):
        first = pl.multiple_of(b * 8, 8)
        rows = lax.broadcasted_iota(jnp.int32, (8, WIDE), 0) + first
        count = jnp.zeros((8, WIDE), F32)
        for n in range(6):
            count = count + jnp.where(near[n : n + 1, :] == rows, 1.0, 0.0)
        matrix32[pl.ds(first, 8), :] = count
        return 0

    lax.fori_loop(0, WIDE // 8, link_rows, 0)
    degree = jnp.zeros((1, WIDE), F32)
    for b in range(WIDE // 128):
        both = matrix32[128 * b : 128 * b + 128, :] + matrix32[:, 128 * b : 128 * b + 128].T
        matrix[128 * b : 128 * b + 128, :] = both.astype(BF16)
        degree = degree + jnp.sum(both, axis=0, keepdims=True)
    inside = lax.broadcasted_iota(jnp.int32, (1, WIDE), 1) < vertices
    diagonal[...] = jnp.where(inside, degree + TETHER_GAIN, 0.0)
    shapes[...] = jnp.zeros_like(shapes)
    flat_tail[...] = jnp.zeros_like(flat_tail)
    for c in range(3):
        shapes[4 * c : 4 * c + 4, 0:vertices] = jnp.broadcast_to(shape_ref[c : c + 1, :], (4, vertices))

    def unfold(from_ref, g, put_rows):
        put_rows(0, 0, MAIN, from_ref[g, 0:4, 0:MAIN])
        put_rows(1, 0, MAIN, from_ref[g, 4:8, 0:MAIN])
        put_rows(2, 0, 256, from_ref[g, 0:4, 640:896])
        put_rows(2, 256, 512, from_ref[g, 4:8, 640:896])
        put_rows(2, 512, MAIN, from_ref[g, 0:4, 896:1024])

    def arrive(g):
        def put_rows(c, first, last, value):
            cells[g, 4 * c : 4 * c + 4, first:last] = value

        unfold(received, g, put_rows)
        tail = received[g, 4:8, 896:1024]
        stiff = jnp.broadcast_to(tail[:, 6:7], (4, 128))
        lanes = lax.broadcasted_iota(jnp.int32, (4, 128), 1)
        for c in range(3):
            end = pltpu.roll(tail, 128 - 2 * c, 1) if c else tail
            cells[g, 4 * c : 4 * c + 4, MAIN:WIDE] = jnp.where(lanes < 2, end, stiff)
        cells[g, 12:16, :] = jnp.zeros((4, WIDE), F32)

    def batch_force(first, many):
        rows = 16 * many
        x = cells[first : first + many].reshape(rows, WIDE)
        keep = lax.broadcasted_iota(jnp.int32, (rows, WIDE), 1) < vertices
        center = jnp.sum(jnp.where(keep, x, 0.0), axis=1, keepdims=True) * (1.0 / vertices)
        shape = jnp.concatenate([shapes[...]] * many, axis=0)
        strain = jnp.where(keep, x - center - shape, 0.0)
        parts = jnp.dot(
            jnp.concatenate(cut(strain), axis=0), matrix[...], preferred_element_type=F32
        )
        linked = parts[0:rows] + parts[rows : 2 * rows] + parts[2 * rows : 3 * rows]
        pulled = strain * diagonal[...] - linked
        forces[first : first + many] = (-x[:, vertices : vertices + 1] * pulled).reshape(many, 16, WIDE)

    def flatten(block, g, row):
        lane = lax.broadcasted_iota(jnp.int32, (1, 128), 1)
        for c in range(3):
            tail = jnp.zeros((1, 128), F32)
            for r in range(CAP):
                flat[g, row + c : row + c + 1, MAIN * r : MAIN * r + MAIN] = block[
                    4 * c + r : 4 * c + r + 1, 0:MAIN
                ]
                end = block[4 * c + r : 4 * c + r + 1, MAIN:WIDE]
                if r:
                    end = pltpu.roll(end, 2 * r, 1)
                tail = jnp.where((lane >= 2 * r) & (lane < 2 * r + 2), end, tail)
            tail = pltpu.roll(tail, 8 * g, 1)
            mine = (lane >= 8 * g) & (lane < 8 * g + 8)
            flat_tail[row + c : row + c + 1, :] = jnp.where(mine, tail, flat_tail[row + c : row + c + 1, :])

    def tabulate(read, put_table, put_lifted, at):
        y = read(1, at)
        low = y < HALF
        along_x = hat(read(0, at), 32, 0.0)
        along_y = hat(y, 32, 0.0)
        along_z = hat_z(read(2, at))
        for j in range(32):
            put_table(j, at, (along_y[j : j + 1] * along_z).astype(BF16))
        along_y = hat(jnp.where(low, y, y - HALF), 24, 0.0)
        for j in range(HALF + 1):
            window[CZ * j : CZ * j + CZ, at] = (along_y[j : j + 1] * along_z).astype(BF16)
        for c in range(3):
            force = read(3 + c, at)
            put_lifted(c, at, (jnp.where(low, force, 0.0) * along_x).astype(BF16))
            put_lifted(3 + c, at, (jnp.where(low, 0.0, force) * along_x).astype(BF16))

    def put_lifted(c, at, value):
        lifted[32 * c : 32 * c + 32, at] = value

    def spread_group(g):
        flatten(cells[g], g, 0)
        flatten(forces[g], g, 3)

        def put_table(j, at, value):
            table[g, 16 * j : 16 * j + 16, at] = value

        for t in range(0, LANES, 128):
            tabulate(lambda n, at: flat[g, n : n + 1, at], put_table, put_lifted, slice(t, t + 128))
        turned[0:WINDOW, 0:192] += lax.dot_general(
            window[...], lifted[...], (((1,), (1,)), ((), ())), preferred_element_type=F32
        )

    def spread_tail():
        def put_table(j, at, value):
            table_tail[16 * j : 16 * j + 16, at] = value

        at = slice(0, 128)
        tabulate(lambda n, at: flat_tail[n : n + 1, at], put_table, put_lifted, at)
        turned[0:WINDOW, 0:192] += lax.dot_general(
            window[:, at], lifted[:, at], (((1,), (1,)), ((), ())), preferred_element_type=F32
        )

    def drifts(picked, row):
        along_x = hat(row, 32, 0.0)
        return [
            jnp.sum(picked[32 * c : 32 * c + 32] * along_x, axis=0, keepdims=True) for c in range(3)
        ]

    def sample_tail():
        picked = jnp.dot(velocity[...], table_tail[...], preferred_element_type=F32)
        used = lax.broadcasted_iota(jnp.int32, (1, 128), 1) < 8 * GROUPS
        for c, value in enumerate(drifts(picked, flat_tail[0:1, :])):
            flat_tail[3 + c : 4 + c, :] = jnp.where(used, value, 0.0)

    def sample_group(g, add):
        lane = lax.broadcasted_iota(jnp.int32, (1, 128), 1)
        for start, width in CHUNKS:
            at = slice(start, start + width)
            picked = jnp.dot(velocity[...], table[g, :, at], preferred_element_type=F32)
            for c, value in enumerate(drifts(picked, flat[g, 0:1, at])):
                flat[g, 3 + c : 4 + c, at] = value
        for c in range(3):
            tail = pltpu.roll(flat_tail[3 + c : 4 + c, :], 128 - 8 * g, 1)
            for r in range(CAP):
                row = slice(4 * c + r, 4 * c + r + 1)
                step = flat[g, 3 + c : 4 + c, MAIN * r : MAIN * r + MAIN]
                end = tail if r == 0 else pltpu.roll(tail, 128 - 2 * r, 1)
                end = jnp.where(lane < 2, end, 0.0)
                if add:
                    drift[g, row, 0:MAIN] += step
                    drift[g, row, MAIN:WIDE] += end
                else:
                    drift[g, row, 0:MAIN] = step
                    drift[g, row, MAIN:WIDE] = end
                    cells[g, row, 0:MAIN] += step
                    cells[g, row, MAIN:WIDE] += end

    def give_back(into, g):
        fold(into, g, lambda c, first, last: drift[g, 4 * c : 4 * c + 4, first:last])
        lanes = lax.broadcasted_iota(jnp.int32, (4, 128), 1)
        ends = [drift[g, 4 * c : 4 * c + 4, MAIN:WIDE] for c in range(3)]
        into[g, 4:8, 896:1024] = jnp.where(
            lanes < 2, ends[0], jnp.where(lanes < 4, pltpu.roll(ends[1], 2, 1), pltpu.roll(ends[2], 4, 1))
        )

    def collide(from_ref):
        def rows(i, _):
            at_x = pl.ds(pl.multiple_of(8 * i, 8), 8)
            for t in range(0, 512, 128):
                at = slice(t, t + 128)
                f = [from_ref[q, at_x, at] for q in range(19)]
                push = [
                    PUSH_SCALE * total[pl.ds(pl.multiple_of(32 * c + 8 * i, 8), 8), at]
                    for c in range(3)
                ]
                density, momentum = moments(f)
                inverse = 1.0 / density
                u = [(momentum[c] + 0.5 * push[c]) * inverse for c in range(3)]
                square = u[0] * u[0] + u[1] * u[1] + u[2] * u[2]
                dot = u[0] * push[0] + u[1] * push[1] + u[2] * push[2]
                rate = RELAX_RATE * density
                half = 1.0 - 0.5 * RELAX_RATE
                base = rate * (1.0 - 1.5 * square) - (3.0 * half) * dot
                for q in range(19):
                    value = base
                    if q:
                        a = signed_sum([(VELOCITY[q][c], u[c]) for c in range(3)])
                        p = signed_sum([(VELOCITY[q][c], push[c]) for c in range(3)])
                        value = base + rate * a * (3.0 + 4.5 * a) + (half * p) * (3.0 + 9.0 * a)
                    post[q, at_x, at] = (1.0 - RELAX_RATE) * f[q] + WEIGHT[q] * value
            return 0

        lax.fori_loop(0, 4, rows, 0)

    def halo_copies(step):
        ends = (
            [(x_send, x_recv, side, (1, 0) if side == 0 else (-1, 0)) for side in range(2)]
            + [(y_send, y_recv, side, (0, 1) if side == 0 else (0, -1)) for side in range(2)]
            + [
                (e_send, e_recv, n, VELOCITY[EDGE_MOVERS[n][0]][:2])
                for n in range(4)
            ]
        )
        return [
            pltpu.make_async_remote_copy(
                src_ref=out.at[step, n],
                dst_ref=into.at[step, n],
                send_sem=halo_send_sem.at[8 * step + k],
                recv_sem=halo_recv_sem.at[8 * step + k],
                device_id=away(dx, dy),
                device_id_type=MESH,
            )
            for k, (out, into, n, (dx, dy)) in enumerate(ends)
        ]

    def exchange(step):
        lane = lax.broadcasted_iota(jnp.int32, (32, 128), 1)
        for n, (q, row, column) in enumerate(EDGE_MOVERS):
            e_send[step, n] = post[q, row : row + 8, column : column + 128]
        for side, (movers, row) in enumerate(((RIGHT_MOVERS, 31), (LEFT_MOVERS, 0))):
            x_send[step, side] = jnp.zeros((8, 512), F32)
            for n, q in enumerate(movers):
                x_send[step, side, n : n + 1, :] = post[q, row : row + 1, :]
        for side, (movers, column, turn) in enumerate(
            ((UPWARD_MOVERS, 384, 16), (DOWNWARD_MOVERS, 0, 0))
        ):
            face = jnp.zeros((32, 128), F32)
            for n, q in enumerate(movers):
                value = post[q, :, column : column + 128]
                shift = (16 * n + turn) % 128
                if shift:
                    value = pltpu.roll(value, shift, 1)
                face = jnp.where((lane >= 16 * n) & (lane < 16 * n + 16), value, face)
            y_send[step, side] = face
        copies = halo_copies(step)
        for copy in copies:
            copy.start()
        return copies

    def shift_rows(value, dx, edge):
        row = lax.broadcasted_iota(jnp.int32, value.shape, 0)
        if dx > 0:
            return jnp.where(row == 0, edge, pltpu.roll(value, 1, 0))
        return jnp.where(row == 31, edge, pltpu.roll(value, 31, 0))

    def shift_layers(value, dz):
        if dz == 0:
            return value
        width = value.shape[1]
        layer = lax.broadcasted_iota(jnp.int32, value.shape, 1) % CZ
        rim, wrap = (0, width + 1 - CZ) if dz > 0 else (CZ - 1, CZ - 1)
        near_by = pltpu.roll(value, 1 if dz > 0 else width - 1, 1)
        return jnp.where(layer == rim, pltpu.roll(value, wrap, 1), near_by)

    def stream(step, copies):
        for q in range(19):
            dx, dy, dz = VELOCITY[q]
            value = post[q]
            if dx:
                value = pltpu.roll(value, 1 if dx > 0 else 31, 0)
            if dy:
                value = pltpu.roll(value, CZ if dy > 0 else 512 - CZ, 1)
            pops[q] = shift_layers(value, dz)
        for copy in copies:
            copy.wait()
        lane = lax.broadcasted_iota(jnp.int32, (32, 128), 1)
        for q in range(19):
            dx, dy, dz = VELOCITY[q]
            if dx:
                side = 0 if dx > 0 else 1
                n = (RIGHT_MOVERS, LEFT_MOVERS)[side].index(q)
                row = 0 if dx > 0 else 31
                edge = x_recv[step, side, n : n + 1, :]
                if dy:
                    edge = pltpu.roll(edge, CZ if dy > 0 else 512 - CZ, 1)
                pops[q, row : row + 1, :] = shift_layers(edge, dz)
            if dy:
                side = 0 if dy > 0 else 1
                n = (UPWARD_MOVERS, DOWNWARD_MOVERS)[side].index(q)
                rim = y_recv[step, side]
                turn = (128 - 16 * n) % 128 if dy > 0 else 112 - 16 * n
                if turn:
                    rim = pltpu.roll(rim, turn, 1)
                if dx:
                    at = [m[0] for m in EDGE_MOVERS].index(q)
                    row = 7 if dx > 0 else 0
                    edge = pltpu.roll(e_recv[step, at], 16 if dy > 0 else 112, 1)
                    rim = shift_rows(rim, dx, edge[row : row + 1, :])
                rim = shift_layers(rim, dz)
                if dy > 0:
                    pops[q, :, 0:128] = jnp.where(lane < CZ, rim, pops[q, :, 0:128])
                else:
                    pops[q, :, 384:512] = jnp.where(lane >= 128 - CZ, rim, pops[q, :, 384:512])

        def rows(i, _):
            at_x = pl.ds(pl.multiple_of(16 * i, 16), 16)
            for t in range(0, 512, 128):
                at = slice(t, t + 128)
                density, momentum = moments([pops[q, at_x, at] for q in range(19)])
                inverse = 1.0 / density
                for c in range(3):
                    rows_c = pl.ds(pl.multiple_of(32 * c + 16 * i, 16), 16)
                    push = PUSH_SCALE * total[rows_c, at]
                    velocity[rows_c, at] = ((momentum[c] + 0.5 * push) * inverse).astype(BF16)
            return 0

        lax.fori_loop(0, 2, rows, 0)

    for step in range(STEPS):
        turned[...] = jnp.zeros_like(turned)
        for first, many in BATCHES if step == 0 else [(0, GROUPS)]:
            if step == 0:
                for g in range(first, first + many):
                    if g != SELF:
                        cell_copy(g).wait_recv()
                    arrive(g)
            batch_force(first, many)

            def one_spread(g, _):
                spread_group(g)
                return 0

            lax.fori_loop(first, first + many, one_spread, 0)
        spread_tail()
        grid = turned[...].T
        total[:, 0:256] = grid[0:96, 0:256]
        total[:, 256:384] = grid[96:192, 0:128] + grid[0:96, 256:384]
        total[:, 384:512] = grid[96:192, 128:256]
        if step == 0:
            load.wait()
        collide(pops)
        copies = exchange(step)
        stream(step, copies)
        sample_tail()
        if step < STEPS - 1:

            def one_sample(g, _):
                sample_group(g, False)
                return 0

            lax.fori_loop(0, GROUPS, one_sample, 0)
        else:
            store_pops = pltpu.make_async_copy(pops, pops_out, local_sem.at[1])
            store_pops.start()
            stores = [
                pltpu.make_async_copy(total.at[32 * c : 32 * c + 32], density_out.at[c], local_sem.at[2 + c])
                for c in range(3)
            ]
            for store in stores:
                store.start()

            def last_sample(i, _):
                g = GROUPS - 1 - i
                sample_group(g, True)
                give_back(backbuf, g)
                back_copy(g).start()
                return 0

            lax.fori_loop(0, GROUPS - 1, last_sample, 0)
            sample_group(SELF, True)
            give_back(returned, SELF)

    for g in range(GROUPS):
        if g != SELF:
            back_copy(g).wait_recv()
    for g in range(GROUPS):

        def put_rows(c, first, last, value):
            gathered[c, 4 * g : 4 * g + 4, first:last] = value

        unfold(returned, g, put_rows)
        tails[4 * g : 4 * g + 4, :] = returned[g, 4:8, 896:1024]
    for c in range(3):
        tail = tails[...]
        gathered[c, :, MAIN:WIDE] = pltpu.roll(tail, 128 - 2 * c, 1) if c else tail
        moved_out[c] = chosen(take, gathered[c])[0:count, 0:vertices]
    store_pops.wait()
    for store in stores:
        store.wait()
    for g in range(GROUPS):
        if g != SELF:
            cell_copy(g).wait_send()
            back_copy(g).wait_send()


def hand_out(a, b, c, a_out, b_out, c_out, a_held, b_held, c_held, in_sems, out_sems):
    pieces = [(a, a_held, a_out, slice(q, min(q + 4, 19))) for q in range(0, 19, 4)]
    pieces += [(b, b_held, b_out, slice(0, 3)), (c, c_held, c_out, slice(0, 3))]
    loads = [
        pltpu.make_async_copy(source.at[at], held.at[at], in_sems.at[n])
        for n, (source, held, _, at) in enumerate(pieces)
    ]
    stores = [
        pltpu.make_async_copy(held.at[at], target.at[at], out_sems.at[n])
        for n, (_, held, target, at) in enumerate(pieces)
    ]
    for load in loads:
        load.start()
    for load, store in zip(loads, stores, strict=True):
        load.wait()
        store.start()
    for store in stores:
        store.wait()


def local(populations, positions, stiffness, membrane_shape, neighbours, home_tile):
    nx = lax.axis_size("gx")
    ny = lax.axis_size("gy")
    places = positions.transpose(1, 0, 2)
    width_x, plane = populations.shape[1:]
    vmem = pl.BlockSpec(memory_space=pltpu.VMEM)
    hbm = pl.BlockSpec(memory_space=pl.ANY)
    populations, moved, density = pl.pallas_call(
        functools.partial(kernel, nx, ny),
        out_shape=(
            jax.ShapeDtypeStruct(populations.shape, F32),
            jax.ShapeDtypeStruct(places.shape, F32),
            jax.ShapeDtypeStruct((3, width_x, plane), F32),
        ),
        in_specs=[hbm] + [vmem] * 5,
        out_specs=(hbm, vmem, hbm),
        scratch_shapes=[
            pltpu.VMEM((GROUPS, 8, MESSAGE), F32),
            pltpu.VMEM((GROUPS, 8, MESSAGE), F32),
            pltpu.VMEM((GROUPS, 8, MESSAGE), F32),
            pltpu.VMEM((GROUPS, 8, MESSAGE), F32),
            pltpu.VMEM((GROUPS, 16, WIDE), F32),
            pltpu.VMEM((GROUPS, 16, WIDE), F32),
            pltpu.VMEM((3, GROUPS * CAP, WIDE), F32),
            pltpu.VMEM((GROUPS * CAP, 128), F32),
            pltpu.VMEM((8, 128), F32),
            pltpu.VMEM((3, 32, WIDE), F32),
            pltpu.VMEM((8, WIDE), jnp.int32),
            pltpu.VMEM((WIDE, WIDE), F32),
            pltpu.VMEM((WIDE, WIDE), BF16),
            pltpu.VMEM((1, WIDE), F32),
            pltpu.VMEM((16, WIDE), F32),
            pltpu.VMEM((GROUPS, 16, WIDE), F32),
            pltpu.VMEM((GROUPS, 8, LANES), F32),
            pltpu.VMEM((8, 128), F32),
            pltpu.VMEM((GROUPS, plane, LANES), BF16),
            pltpu.VMEM((plane, 128), BF16),
            pltpu.VMEM((WINDOW, LANES), BF16),
            pltpu.VMEM((6 * width_x, LANES), BF16),
            pltpu.VMEM((3 * width_x, plane), F32),
            pltpu.VMEM((384, 256), F32),
            pltpu.VMEM(populations.shape, F32),
            pltpu.VMEM(populations.shape, F32),
            pltpu.VMEM((3 * width_x, plane), BF16),
            pltpu.VMEM((STEPS, 2, 8, plane), F32),
            pltpu.VMEM((STEPS, 2, width_x, 128), F32),
            pltpu.VMEM((STEPS, 4, 8, 128), F32),
            pltpu.VMEM((STEPS, 2, 8, plane), F32),
            pltpu.VMEM((STEPS, 2, width_x, 128), F32),
            pltpu.VMEM((STEPS, 4, 8, 128), F32),
            pltpu.SemaphoreType.DMA((GROUPS,)),
            pltpu.SemaphoreType.DMA((GROUPS,)),
            pltpu.SemaphoreType.DMA((GROUPS,)),
            pltpu.SemaphoreType.DMA((GROUPS,)),
            pltpu.SemaphoreType.DMA((8 * STEPS,)),
            pltpu.SemaphoreType.DMA((8 * STEPS,)),
            pltpu.SemaphoreType.DMA((5,)),
        ],
        compiler_params=pltpu.CompilerParams(
            collective_id=0, has_side_effects=True, vmem_limit_bytes=58 * 2**20
        ),
    )(populations, places, stiffness[None], home_tile[None], membrane_shape, neighbours.T)
    results = (populations, moved, density)
    populations, moved, density = pl.pallas_call(
        hand_out,
        out_shape=tuple(jax.ShapeDtypeStruct(r.shape, F32) for r in results),
        in_specs=[hbm] * 3,
        out_specs=(hbm,) * 3,
        scratch_shapes=[pltpu.VMEM(r.shape, F32) for r in results]
        + [pltpu.SemaphoreType.DMA((7,)), pltpu.SemaphoreType.DMA((7,))],
    )(*results)
    return populations, moved.transpose(1, 0, 2), density


def solution(mesh):
    placed = (
        P(None, "gx", "gy"),
        P(("gx", "gy"), None, None),
        P(("gx", "gy")),
        P(),
        P(),
        P(("gx", "gy")),
    )
    return jax.shard_map(
        local,
        mesh=mesh,
        in_specs=placed,
        out_specs=(P(None, "gx", "gy"), P(("gx", "gy"), None, None), P(None, "gx", "gy")),
        check_vma=False,
    )
```

```python
import functools

import jax
import jax.numpy as jnp
from jax import lax
from jax.experimental import pallas as pl
from jax.experimental.pallas import tpu as pltpu
from jax.sharding import PartitionSpec as P

CZ = 16
CAP = 4
STEPS = 2
GROUPS = 12
SELF = 0
BATCHES = [(0, 1), (1, 2), (3, 3), (9, 3), (6, 3)]
WIDE = 768
MAIN = 640
LANES = CAP * MAIN
MESSAGE = 1024
HALF = 16
WINDOW = (HALF + 1) * CZ
CHUNKS = [(start, 512) for start in range(0, LANES, 512)]

VELOCITY = [
    (0, 0, 0),
    (1, 0, 0),
    (-1, 0, 0),
    (0, 1, 0),
    (0, -1, 0),
    (0, 0, 1),
    (0, 0, -1),
    (1, 1, 0),
    (-1, -1, 0),
    (1, -1, 0),
    (-1, 1, 0),
    (1, 0, 1),
    (-1, 0, -1),
    (1, 0, -1),
    (-1, 0, 1),
    (0, 1, 1),
    (0, -1, -1),
    (0, 1, -1),
    (0, -1, 1),
]
WEIGHT = [1.0 / 3.0] + [1.0 / 18.0] * 6 + [1.0 / 36.0] * 12
RIGHT_MOVERS = [1, 7, 9, 11, 13]
LEFT_MOVERS = [2, 8, 10, 12, 14]
UPWARD_MOVERS = [3, 7, 10, 15, 17]
DOWNWARD_MOVERS = [4, 8, 9, 16, 18]
EDGE_MOVERS = [(7, 24, 384), (8, 0, 0), (9, 24, 0), (10, 0, 384)]
RELAX_RATE = 1.25
PUSH_SCALE = 0.05
TETHER_GAIN = 2.0
MESH = pl.DeviceIdType.MESH
F32 = jnp.float32
BF16 = jnp.bfloat16


def signed_sum(parts):
    total = None
    for sign, value in parts:
        if sign == 0:
            continue
        if total is None:
            total = value if sign > 0 else -value
        else:
            total = total + value if sign > 0 else total - value
    return total


def moments(f):
    density = f[0]
    for q in range(1, 19):
        density = density + f[q]
    momentum = [signed_sum([(VELOCITY[q][c], f[q]) for q in range(1, 19)]) for c in range(3)]
    return density, momentum


def hat(row, count, first):
    grid = lax.broadcasted_iota(jnp.int32, (count, row.shape[1]), 0).astype(F32) + first
    return jnp.maximum(0.0, 1.0 - jnp.abs(row - grid))


def hat_z(row):
    wrapped = row - CZ * jnp.floor(row * (1.0 / CZ))
    grid = lax.broadcasted_iota(jnp.int32, (CZ, row.shape[1]), 0).astype(F32)
    gap = jnp.abs(wrapped - grid)
    return jnp.maximum(0.0, 1.0 - jnp.minimum(gap, CZ - gap))


def cut(value):
    high = value.astype(BF16)
    rest = value - high.astype(F32)
    middle = rest.astype(BF16)
    return high, middle, (rest - middle.astype(F32)).astype(BF16)


def chosen(choice, rows):
    parts = [jnp.dot(choice, part, preferred_element_type=F32) for part in cut(rows)]
    return (parts[0] + parts[1]) + parts[2]


def kernel(
    nx,
    ny,
    pops_ref,
    places_ref,
    stiff_ref,
    home_ref,
    shape_ref,
    near_ref,
    pops_out,
    moved_out,
    density_out,
    sendbuf,
    received,
    backbuf,
    returned,
    cells,
    drift,
    gathered,
    tails,
    cell_rows,
    places_pad,
    near,
    matrix32,
    matrix,
    diagonal,
    shapes,
    forces,
    flat,
    flat_tail,
    table,
    table_tail,
    lifted,
    total,
    turned,
    pops,
    post,
    velocity,
    windows,
    x_send,
    y_send,
    e_send,
    x_recv,
    y_recv,
    e_recv,
    cell_send_sem,
    cell_recv_sem,
    back_send_sem,
    back_recv_sem,
    halo_send_sem,
    halo_recv_sem,
    local_sem,
):
    load = pltpu.make_async_copy(pops_ref, pops, local_sem.at[0])
    load.start()
    me_x = lax.axis_index("gx")
    me_y = lax.axis_index("gy")
    vertices = places_ref.shape[2]
    near[...] = jnp.full((8, WIDE), -1, jnp.int32)
    near[0:6, 0:vertices] = near_ref[...]

    def away(dx, dy):
        return (lax.rem(me_x + dx + nx, nx), lax.rem(me_y + dy + ny, ny))

    barrier = pltpu.get_barrier_semaphore()
    for g in range(GROUPS):
        if g != SELF:
            pl.semaphore_signal(barrier, inc=1, device_id=away((g % 3 + 1) % 3 - 1, g // 3), device_id_type=MESH)

    count = places_ref.shape[1]
    cell_rows[...] = jnp.full((8, 128), -1.0, F32)
    cell_rows[0:1, 0:count] = home_ref[...].astype(F32)
    cell_rows[1:2, 0:count] = stiff_ref[...]
    home = jnp.broadcast_to(cell_rows[0:1, :], (128, 128))
    across = lax.broadcasted_iota(jnp.int32, (128, 128), 1)
    down = lax.broadcasted_iota(jnp.int32, (128, 128), 0)
    earlier = (home == home.T) & (down < across)
    rank = jnp.sum(jnp.where(earlier, 1.0, 0.0), axis=0, keepdims=True)
    home = cell_rows[0:1, :]
    tile_x = jnp.floor((home + 0.5) * (1.0 / ny))
    offset = tile_x - (me_x - 1).astype(F32)
    offset = jnp.where(offset < 0, offset + nx, offset)
    offset = jnp.where(offset >= nx, offset - nx, offset)
    turn = home - ny * tile_x - me_y.astype(F32)
    turn = jnp.where(turn < 0, turn + ny, turn)
    lane = lax.broadcasted_iota(jnp.int32, (1, 128), 1)
    side = jnp.where(offset < 1, offset + 2, offset - 1)
    slot = jnp.where(lane < count, (turn * 3 + side) * CAP + rank, -1.0)
    hit = jnp.where(slot == down.astype(F32), 1.0, 0.0)
    put = hit[0 : GROUPS * CAP, 0:32].astype(BF16)
    take = hit.T[0:32, 0 : GROUPS * CAP].astype(BF16)
    stiff = jnp.sum(hit * cell_rows[1:2, :], axis=1, keepdims=True)[0 : GROUPS * CAP]
    places_pad[...] = jnp.zeros_like(places_pad)
    for c in range(3):
        places_pad[c, 0:count, 0:vertices] = places_ref[c]
        gathered[c] = chosen(put, places_pad[c])
    lanes = lax.broadcasted_iota(jnp.int32, (GROUPS * CAP, 128), 1)
    tails[...] = jnp.where(
        lanes < 2,
        gathered[0, :, MAIN:WIDE],
        jnp.where(
            lanes < 4,
            pltpu.roll(gathered[1, :, MAIN:WIDE], 2, 1),
            jnp.where(lanes < 6, pltpu.roll(gathered[2, :, MAIN:WIDE], 4, 1), stiff),
        ),
    )

    def fold(into, at, rows):
        into[at, 0:4, 0:MAIN] = rows(0, 0, MAIN)
        into[at, 4:8, 0:MAIN] = rows(1, 0, MAIN)
        into[at, 0:4, 640:896] = rows(2, 0, 256)
        into[at, 4:8, 640:896] = rows(2, 256, 512)
        into[at, 0:4, 896:1024] = rows(2, 512, MAIN)

    for g in range(GROUPS):
        into = received if g == SELF else sendbuf
        fold(into, g, lambda c, first, last, g=g: gathered[c, 4 * g : 4 * g + 4, first:last])
        into[g, 4:8, 896:1024] = tails[4 * g : 4 * g + 4, :]
    pl.semaphore_wait(barrier, GROUPS - 1)

    def cell_copy(g):
        return pltpu.make_async_remote_copy(
            src_ref=sendbuf.at[g],
            dst_ref=received.at[g],
            send_sem=cell_send_sem.at[g],
            recv_sem=cell_recv_sem.at[g],
            device_id=away((g % 3 + 1) % 3 - 1, g // 3),
            device_id_type=MESH,
        )

    def back_copy(g):
        return pltpu.make_async_remote_copy(
            src_ref=backbuf.at[g],
            dst_ref=returned.at[g],
            send_sem=back_send_sem.at[g],
            recv_sem=back_recv_sem.at[g],
            device_id=away(1 - (g % 3 + 1) % 3, ny - g // 3),
            device_id_type=MESH,
        )

    for g in (1, 2, 3, 9, 4, 10, 5, 11, 6, 7, 8):
        cell_copy(g).start()

    def link_rows(b, _):
        first = pl.multiple_of(b * 8, 8)
        rows = lax.broadcasted_iota(jnp.int32, (8, WIDE), 0) + first
        count = jnp.zeros((8, WIDE), F32)
        for n in range(6):
            count = count + jnp.where(near[n : n + 1, :] == rows, 1.0, 0.0)
        matrix32[pl.ds(first, 8), :] = count
        return 0

    lax.fori_loop(0, WIDE // 8, link_rows, 0)
    degree = jnp.zeros((1, WIDE), F32)
    for b in range(WIDE // 128):
        both = matrix32[128 * b : 128 * b + 128, :] + matrix32[:, 128 * b : 128 * b + 128].T
        matrix[128 * b : 128 * b + 128, :] = both.astype(BF16)
        degree = degree + jnp.sum(both, axis=0, keepdims=True)
    inside = lax.broadcasted_iota(jnp.int32, (1, WIDE), 1) < vertices
    diagonal[...] = jnp.where(inside, degree + TETHER_GAIN, 0.0)
    shapes[...] = jnp.zeros_like(shapes)
    flat_tail[...] = jnp.zeros_like(flat_tail)
    for c in range(3):
        shapes[4 * c : 4 * c + 4, 0:vertices] = jnp.broadcast_to(shape_ref[c : c + 1, :], (4, vertices))

    def unfold(from_ref, g, put_rows):
        put_rows(0, 0, MAIN, from_ref[g, 0:4, 0:MAIN])
        put_rows(1, 0, MAIN, from_ref[g, 4:8, 0:MAIN])
        put_rows(2, 0, 256, from_ref[g, 0:4, 640:896])
        put_rows(2, 256, 512, from_ref[g, 4:8, 640:896])
        put_rows(2, 512, MAIN, from_ref[g, 0:4, 896:1024])

    def arrive(g):
        def put_rows(c, first, last, value):
            cells[g, 4 * c : 4 * c + 4, first:last] = value

        unfold(received, g, put_rows)
        tail = received[g, 4:8, 896:1024]
        stiff = jnp.broadcast_to(tail[:, 6:7], (4, 128))
        lanes = lax.broadcasted_iota(jnp.int32, (4, 128), 1)
        for c in range(3):
            end = pltpu.roll(tail, 128 - 2 * c, 1) if c else tail
            cells[g, 4 * c : 4 * c + 4, MAIN:WIDE] = jnp.where(lanes < 2, end, stiff)
        cells[g, 12:16, :] = jnp.zeros((4, WIDE), F32)

    def batch_force(first, many):
        rows = 16 * many
        x = cells[first : first + many].reshape(rows, WIDE)
        keep = lax.broadcasted_iota(jnp.int32, (rows, WIDE), 1) < vertices
        center = jnp.sum(jnp.where(keep, x, 0.0), axis=1, keepdims=True) * (1.0 / vertices)
        shape = jnp.concatenate([shapes[...]] * many, axis=0)
        strain = jnp.where(keep, x - center - shape, 0.0)
        parts = jnp.dot(
            jnp.concatenate(cut(strain), axis=0), matrix[...], preferred_element_type=F32
        )
        linked = parts[0:rows] + parts[rows : 2 * rows] + parts[2 * rows : 3 * rows]
        pulled = strain * diagonal[...] - linked
        forces[first : first + many] = (-x[:, vertices : vertices + 1] * pulled).reshape(many, 16, WIDE)

    def flatten(block, g, row):
        lane = lax.broadcasted_iota(jnp.int32, (1, 128), 1)
        for c in range(3):
            tail = jnp.zeros((1, 128), F32)
            for r in range(CAP):
                flat[g, row + c : row + c + 1, MAIN * r : MAIN * r + MAIN] = block[
                    4 * c + r : 4 * c + r + 1, 0:MAIN
                ]
                end = block[4 * c + r : 4 * c + r + 1, MAIN:WIDE]
                if r:
                    end = pltpu.roll(end, 2 * r, 1)
                tail = jnp.where((lane >= 2 * r) & (lane < 2 * r + 2), end, tail)
            tail = pltpu.roll(tail, 8 * g, 1)
            mine = (lane >= 8 * g) & (lane < 8 * g + 8)
            flat_tail[row + c : row + c + 1, :] = jnp.where(mine, tail, flat_tail[row + c : row + c + 1, :])

    def tabulate(read, put_table, put_lifted, at):
        y = read(1, at)
        low = y < HALF
        along_x = hat(read(0, at), 32, 0.0)
        along_y = hat(jnp.where(low, y, y - HALF), 24, 0.0)
        along_z = hat_z(read(2, at))
        for j in range(HALF + 1):
            put_table(j, at, (along_y[j : j + 1] * along_z).astype(BF16))
        for c in range(3):
            force = read(3 + c, at)
            put_lifted(c, at, (jnp.where(low, force, 0.0) * along_x).astype(BF16))
            put_lifted(3 + c, at, (jnp.where(low, 0.0, force) * along_x).astype(BF16))

    def put_lifted(c, at, value):
        lifted[32 * c : 32 * c + 32, at] = value

    def spread_group(g):
        flatten(cells[g], g, 0)
        flatten(forces[g], g, 3)

        def put_table(j, at, value):
            table[g, 16 * j : 16 * j + 16, at] = value

        for t in range(0, LANES, 128):
            tabulate(lambda n, at: flat[g, n : n + 1, at], put_table, put_lifted, slice(t, t + 128))
        turned[0:WINDOW, 0:192] += lax.dot_general(
            table[g], lifted[...], (((1,), (1,)), ((), ())), preferred_element_type=F32
        )

    def spread_tail():
        def put_table(j, at, value):
            table_tail[16 * j : 16 * j + 16, at] = value

        at = slice(0, 128)
        tabulate(lambda n, at: flat_tail[n : n + 1, at], put_table, put_lifted, at)
        turned[0:WINDOW, 0:192] += lax.dot_general(
            table_tail[...], lifted[:, at], (((1,), (1,)), ((), ())), preferred_element_type=F32
        )

    def drifts(picked, x, y):
        along_x = hat(x, 32, 0.0)
        low = y < HALF
        return [
            jnp.sum(
                jnp.where(low, picked[32 * c : 32 * c + 32], picked[96 + 32 * c : 128 + 32 * c]) * along_x,
                axis=0,
                keepdims=True,
            )
            for c in range(3)
        ]

    def sample_tail():
        picked = jnp.dot(windows[:, 0:WINDOW], table_tail[...], preferred_element_type=F32)
        used = lax.broadcasted_iota(jnp.int32, (1, 128), 1) < 8 * GROUPS
        for c, value in enumerate(drifts(picked, flat_tail[0:1, :], flat_tail[1:2, :])):
            flat_tail[3 + c : 4 + c, :] = jnp.where(used, value, 0.0)

    def sample_group(g, add):
        lane = lax.broadcasted_iota(jnp.int32, (1, 128), 1)
        for start, width in CHUNKS:
            at = slice(start, start + width)
            picked = jnp.dot(
                windows[:, 0:256], table[g, 0:256, at], preferred_element_type=F32
            ) + jnp.dot(windows[:, 256:WINDOW], table[g, 256:WINDOW, at], preferred_element_type=F32)
            for c, value in enumerate(drifts(picked, flat[g, 0:1, at], flat[g, 1:2, at])):
                flat[g, 3 + c : 4 + c, at] = value
        for c in range(3):
            tail = pltpu.roll(flat_tail[3 + c : 4 + c, :], 128 - 8 * g, 1)
            for r in range(CAP):
                row = slice(4 * c + r, 4 * c + r + 1)
                step = flat[g, 3 + c : 4 + c, MAIN * r : MAIN * r + MAIN]
                end = tail if r == 0 else pltpu.roll(tail, 128 - 2 * r, 1)
                end = jnp.where(lane < 2, end, 0.0)
                if add:
                    drift[g, row, 0:MAIN] += step
                    drift[g, row, MAIN:WIDE] += end
                else:
                    drift[g, row, 0:MAIN] = step
                    drift[g, row, MAIN:WIDE] = end
                    cells[g, row, 0:MAIN] += step
                    cells[g, row, MAIN:WIDE] += end

    def give_back(into, g):
        fold(into, g, lambda c, first, last: drift[g, 4 * c : 4 * c + 4, first:last])
        lanes = lax.broadcasted_iota(jnp.int32, (4, 128), 1)
        ends = [drift[g, 4 * c : 4 * c + 4, MAIN:WIDE] for c in range(3)]
        into[g, 4:8, 896:1024] = jnp.where(
            lanes < 2, ends[0], jnp.where(lanes < 4, pltpu.roll(ends[1], 2, 1), pltpu.roll(ends[2], 4, 1))
        )

    def collide(from_ref):
        def rows(i, _):
            at_x = pl.ds(pl.multiple_of(8 * i, 8), 8)
            for t in range(0, 512, 128):
                at = slice(t, t + 128)
                f = [from_ref[q, at_x, at] for q in range(19)]
                push = [
                    PUSH_SCALE * total[pl.ds(pl.multiple_of(32 * c + 8 * i, 8), 8), at]
                    for c in range(3)
                ]
                density, momentum = moments(f)
                inverse = 1.0 / density
                u = [(momentum[c] + 0.5 * push[c]) * inverse for c in range(3)]
                square = u[0] * u[0] + u[1] * u[1] + u[2] * u[2]
                dot = u[0] * push[0] + u[1] * push[1] + u[2] * push[2]
                rate = RELAX_RATE * density
                half = 1.0 - 0.5 * RELAX_RATE
                base = rate * (1.0 - 1.5 * square) - (3.0 * half) * dot
                for q in range(19):
                    value = base
                    if q:
                        a = signed_sum([(VELOCITY[q][c], u[c]) for c in range(3)])
                        p = signed_sum([(VELOCITY[q][c], push[c]) for c in range(3)])
                        value = base + rate * a * (3.0 + 4.5 * a) + (half * p) * (3.0 + 9.0 * a)
                    post[q, at_x, at] = (1.0 - RELAX_RATE) * f[q] + WEIGHT[q] * value
            return 0

        lax.fori_loop(0, 4, rows, 0)

    def halo_copies(step):
        ends = (
            [(x_send, x_recv, side, (1, 0) if side == 0 else (-1, 0)) for side in range(2)]
            + [(y_send, y_recv, side, (0, 1) if side == 0 else (0, -1)) for side in range(2)]
            + [
                (e_send, e_recv, n, VELOCITY[EDGE_MOVERS[n][0]][:2])
                for n in range(4)
            ]
        )
        return [
            pltpu.make_async_remote_copy(
                src_ref=out.at[step, n],
                dst_ref=into.at[step, n],
                send_sem=halo_send_sem.at[8 * step + k],
                recv_sem=halo_recv_sem.at[8 * step + k],
                device_id=away(dx, dy),
                device_id_type=MESH,
            )
            for k, (out, into, n, (dx, dy)) in enumerate(ends)
        ]

    def exchange(step):
        lane = lax.broadcasted_iota(jnp.int32, (32, 128), 1)
        copies = halo_copies(step)
        for n, (q, row, column) in enumerate(EDGE_MOVERS):
            e_send[step, n] = post[q, row : row + 8, column : column + 128]
            copies[4 + n].start()
        for side, (movers, row) in enumerate(((RIGHT_MOVERS, 31), (LEFT_MOVERS, 0))):
            x_send[step, side] = jnp.zeros((8, 512), F32)
            for n, q in enumerate(movers):
                x_send[step, side, n : n + 1, :] = post[q, row : row + 1, :]
            copies[side].start()
        for side, (movers, column, turn) in enumerate(
            ((UPWARD_MOVERS, 384, 16), (DOWNWARD_MOVERS, 0, 0))
        ):
            face = jnp.zeros((32, 128), F32)
            for n, q in enumerate(movers):
                value = post[q, :, column : column + 128]
                shift = (16 * n + turn) % 128
                if shift:
                    value = pltpu.roll(value, shift, 1)
                face = jnp.where((lane >= 16 * n) & (lane < 16 * n + 16), value, face)
            y_send[step, side] = face
            copies[2 + side].start()
        return copies

    def shift_rows(value, dx, edge):
        row = lax.broadcasted_iota(jnp.int32, value.shape, 0)
        if dx > 0:
            return jnp.where(row == 0, edge, pltpu.roll(value, 1, 0))
        return jnp.where(row == 31, edge, pltpu.roll(value, 31, 0))

    def shift_layers(value, dz):
        if dz == 0:
            return value
        width = value.shape[1]
        layer = lax.broadcasted_iota(jnp.int32, value.shape, 1) % CZ
        rim, wrap = (0, width + 1 - CZ) if dz > 0 else (CZ - 1, CZ - 1)
        near_by = pltpu.roll(value, 1 if dz > 0 else width - 1, 1)
        return jnp.where(layer == rim, pltpu.roll(value, wrap, 1), near_by)

    def stream(step, copies):
        for q in range(19):
            dx, dy, dz = VELOCITY[q]
            value = post[q]
            if dx:
                value = pltpu.roll(value, 1 if dx > 0 else 31, 0)
            if dy:
                value = pltpu.roll(value, CZ if dy > 0 else 512 - CZ, 1)
            pops[q] = shift_layers(value, dz)
        for copy in copies:
            copy.wait()
        lane = lax.broadcasted_iota(jnp.int32, (32, 128), 1)
        for q in range(19):
            dx, dy, dz = VELOCITY[q]
            if dx:
                side = 0 if dx > 0 else 1
                n = (RIGHT_MOVERS, LEFT_MOVERS)[side].index(q)
                row = 0 if dx > 0 else 31
                edge = x_recv[step, side, n : n + 1, :]
                if dy:
                    edge = pltpu.roll(edge, CZ if dy > 0 else 512 - CZ, 1)
                pops[q, row : row + 1, :] = shift_layers(edge, dz)
            if dy:
                side = 0 if dy > 0 else 1
                n = (UPWARD_MOVERS, DOWNWARD_MOVERS)[side].index(q)
                rim = y_recv[step, side]
                turn = (128 - 16 * n) % 128 if dy > 0 else 112 - 16 * n
                if turn:
                    rim = pltpu.roll(rim, turn, 1)
                if dx:
                    at = [m[0] for m in EDGE_MOVERS].index(q)
                    row = 7 if dx > 0 else 0
                    edge = pltpu.roll(e_recv[step, at], 16 if dy > 0 else 112, 1)
                    rim = shift_rows(rim, dx, edge[row : row + 1, :])
                rim = shift_layers(rim, dz)
                if dy > 0:
                    pops[q, :, 0:128] = jnp.where(lane < CZ, rim, pops[q, :, 0:128])
                else:
                    pops[q, :, 384:512] = jnp.where(lane >= 128 - CZ, rim, pops[q, :, 384:512])

        def rows(i, _):
            at_x = pl.ds(pl.multiple_of(16 * i, 16), 16)
            for t in range(0, 512, 128):
                at = slice(t, t + 128)
                density, momentum = moments([pops[q, at_x, at] for q in range(19)])
                inverse = 1.0 / density
                for c in range(3):
                    rows_c = pl.ds(pl.multiple_of(32 * c + 16 * i, 16), 16)
                    push = PUSH_SCALE * total[rows_c, at]
                    velocity[rows_c, at] = ((momentum[c] + 0.5 * push) * inverse).astype(BF16)
            return 0

        lax.fori_loop(0, 2, rows, 0)

    for step in range(STEPS):
        turned[...] = jnp.zeros_like(turned)
        for first, many in BATCHES if step == 0 else [(0, GROUPS)]:
            if step == 0:
                for g in range(first, first + many):
                    if g != SELF:
                        cell_copy(g).wait_recv()
                    arrive(g)
            batch_force(first, many)

            def one_spread(g, _):
                spread_group(g)
                return 0

            lax.fori_loop(first, first + many, one_spread, 0)
        spread_tail()
        grid = turned[...].T
        total[:, 0:256] = grid[0:96, 0:256]
        total[:, 256:384] = grid[96:192, 0:128] + grid[0:96, 256:384]
        total[:, 384:512] = grid[96:192, 128:256]
        if step == 0:
            load.wait()
        collide(pops)
        copies = exchange(step)
        stream(step, copies)
        windows[0:96, 0:384] = velocity[:, 0:384]
        windows[96:192, 0:256] = velocity[:, 256:512]
        windows[96:192, 256:384] = jnp.zeros((96, 128), BF16)
        sample_tail()
        if step < STEPS - 1:

            def one_sample(g, _):
                sample_group(g, False)
                return 0

            lax.fori_loop(0, GROUPS, one_sample, 0)
        else:
            store_pops = pltpu.make_async_copy(pops, pops_out, local_sem.at[1])
            store_pops.start()
            stores = [
                pltpu.make_async_copy(total.at[32 * c : 32 * c + 32], density_out.at[c], local_sem.at[2 + c])
                for c in range(3)
            ]
            for store in stores:
                store.start()

            def last_sample(i, _):
                g = GROUPS - 1 - i
                sample_group(g, True)
                give_back(backbuf, g)
                back_copy(g).start()
                return 0

            lax.fori_loop(0, GROUPS - 1, last_sample, 0)
            sample_group(SELF, True)
            give_back(returned, SELF)

    for g in range(GROUPS):
        if g != SELF:
            back_copy(g).wait_recv()
    for g in range(GROUPS):

        def put_rows(c, first, last, value):
            gathered[c, 4 * g : 4 * g + 4, first:last] = value

        unfold(returned, g, put_rows)
        tails[4 * g : 4 * g + 4, :] = returned[g, 4:8, 896:1024]
    for c in range(3):
        tail = tails[...]
        gathered[c, :, MAIN:WIDE] = pltpu.roll(tail, 128 - 2 * c, 1) if c else tail
        moved_out[c] = chosen(take, gathered[c])[0:count, 0:vertices]
    store_pops.wait()
    for store in stores:
        store.wait()
    for g in range(GROUPS):
        if g != SELF:
            cell_copy(g).wait_send()
            back_copy(g).wait_send()


def hand_out(a, b, c, a_out, b_out, c_out, a_held, b_held, c_held, in_sems, out_sems):
    pieces = [(a, a_held, a_out, slice(q, min(q + 4, 19))) for q in range(0, 19, 4)]
    pieces += [(b, b_held, b_out, slice(0, 3)), (c, c_held, c_out, slice(0, 3))]
    loads = [
        pltpu.make_async_copy(source.at[at], held.at[at], in_sems.at[n])
        for n, (source, held, _, at) in enumerate(pieces)
    ]
    stores = [
        pltpu.make_async_copy(held.at[at], target.at[at], out_sems.at[n])
        for n, (_, held, target, at) in enumerate(pieces)
    ]
    for load in loads:
        load.start()
    for load, store in zip(loads, stores, strict=True):
        load.wait()
        store.start()
    for store in stores:
        store.wait()


def local(populations, positions, stiffness, membrane_shape, neighbours, home_tile):
    nx = lax.axis_size("gx")
    ny = lax.axis_size("gy")
    places = positions.transpose(1, 0, 2)
    width_x, plane = populations.shape[1:]
    vmem = pl.BlockSpec(memory_space=pltpu.VMEM)
    hbm = pl.BlockSpec(memory_space=pl.ANY)
    populations, moved, density = pl.pallas_call(
        functools.partial(kernel, nx, ny),
        out_shape=(
            jax.ShapeDtypeStruct(populations.shape, F32),
            jax.ShapeDtypeStruct(places.shape, F32),
            jax.ShapeDtypeStruct((3, width_x, plane), F32),
        ),
        in_specs=[hbm] + [vmem] * 5,
        out_specs=(hbm, vmem, hbm),
        scratch_shapes=[
            pltpu.VMEM((GROUPS, 8, MESSAGE), F32),
            pltpu.VMEM((GROUPS, 8, MESSAGE), F32),
            pltpu.VMEM((GROUPS, 8, MESSAGE), F32),
            pltpu.VMEM((GROUPS, 8, MESSAGE), F32),
            pltpu.VMEM((GROUPS, 16, WIDE), F32),
            pltpu.VMEM((GROUPS, 16, WIDE), F32),
            pltpu.VMEM((3, GROUPS * CAP, WIDE), F32),
            pltpu.VMEM((GROUPS * CAP, 128), F32),
            pltpu.VMEM((8, 128), F32),
            pltpu.VMEM((3, 32, WIDE), F32),
            pltpu.VMEM((8, WIDE), jnp.int32),
            pltpu.VMEM((WIDE, WIDE), F32),
            pltpu.VMEM((WIDE, WIDE), BF16),
            pltpu.VMEM((1, WIDE), F32),
            pltpu.VMEM((16, WIDE), F32),
            pltpu.VMEM((GROUPS, 16, WIDE), F32),
            pltpu.VMEM((GROUPS, 8, LANES), F32),
            pltpu.VMEM((8, 128), F32),
            pltpu.VMEM((GROUPS, WINDOW, LANES), BF16),
            pltpu.VMEM((WINDOW, 128), BF16),
            pltpu.VMEM((6 * width_x, LANES), BF16),
            pltpu.VMEM((3 * width_x, plane), F32),
            pltpu.VMEM((384, 256), F32),
            pltpu.VMEM(populations.shape, F32),
            pltpu.VMEM(populations.shape, F32),
            pltpu.VMEM((3 * width_x, plane), BF16),
            pltpu.VMEM((6 * width_x, 384), BF16),
            pltpu.VMEM((STEPS, 2, 8, plane), F32),
            pltpu.VMEM((STEPS, 2, width_x, 128), F32),
            pltpu.VMEM((STEPS, 4, 8, 128), F32),
            pltpu.VMEM((STEPS, 2, 8, plane), F32),
            pltpu.VMEM((STEPS, 2, width_x, 128), F32),
            pltpu.VMEM((STEPS, 4, 8, 128), F32),
            pltpu.SemaphoreType.DMA((GROUPS,)),
            pltpu.SemaphoreType.DMA((GROUPS,)),
            pltpu.SemaphoreType.DMA((GROUPS,)),
            pltpu.SemaphoreType.DMA((GROUPS,)),
            pltpu.SemaphoreType.DMA((8 * STEPS,)),
            pltpu.SemaphoreType.DMA((8 * STEPS,)),
            pltpu.SemaphoreType.DMA((5,)),
        ],
        compiler_params=pltpu.CompilerParams(
            collective_id=0, has_side_effects=True, vmem_limit_bytes=58 * 2**20
        ),
    )(populations, places, stiffness[None], home_tile[None], membrane_shape, neighbours.T)
    results = (populations, moved, density)
    populations, moved, density = pl.pallas_call(
        hand_out,
        out_shape=tuple(jax.ShapeDtypeStruct(r.shape, F32) for r in results),
        in_specs=[hbm] * 3,
        out_specs=(hbm,) * 3,
        scratch_shapes=[pltpu.VMEM(r.shape, F32) for r in results]
        + [pltpu.SemaphoreType.DMA((7,)), pltpu.SemaphoreType.DMA((7,))],
    )(*results)
    return populations, moved.transpose(1, 0, 2), density


def solution(mesh):
    placed = (
        P(None, "gx", "gy"),
        P(("gx", "gy"), None, None),
        P(("gx", "gy")),
        P(),
        P(),
        P(("gx", "gy")),
    )
    return jax.shard_map(
        local,
        mesh=mesh,
        in_specs=placed,
        out_specs=(P(None, "gx", "gy"), P(("gx", "gy"), None, None), P(None, "gx", "gy")),
        check_vma=False,
    )
```
